32 devices in a mesh: cfg: 2 (over x), req: 4 (over z), seq: 4 (over y, core).
Axes of the slice: x: 2, y: 2, z: 4, core: 2. Of those that a mesh axis runs over, the one named last changes fastest.
Arguments:
- img_state: bfloat16 [2, 8, 1024, 1536], P('cfg', 'req', 'seq'), may hold values from -6 to 6
- txt_state: bfloat16 [2, 8, 192, 1536], P('cfg', 'req', 'seq'), may hold values from -6 to 6
- cond_vec: float32 [2, 8, 1536], P('cfg'), may hold values from -6 to 6
- text_len: int32 [2, 8], P('cfg', 'req'), may hold values from 38 to 154, as said below
- latent: float32 [8, 1024, 64], P('req', 'seq', 'cfg'), may hold values from -6 to 6
- w_mod: bfloat16 [15360, 1536], P(('req', 'seq')), may hold values from -0.15625 to 0.15625
- w_qkv_img: bfloat16 [3, 1536, 1536], P(None, 'seq')
- w_qkv_txt: bfloat16 [3, 1536, 1536], P(None, 'seq')
- w_attn_out: bfloat16 [1536, 1536], P('seq'), may hold values from -2 to 2
- w_up: bfloat16 [6144, 1536], P(('cfg', 'req', 'seq')), may hold values from -0.15625 to 0.15625
- w_down: bfloat16 [6144, 1536], P(('cfg', 'req', 'seq')), may hold values from -0.078125 to 0.078125
- w_final: bfloat16 [1536, 64], replicated, may hold values from -0.078125 to 0.078125
Outputs:
- velocity: float32 [8, 1024, 64], P('req', 'seq', 'cfg')
- latent_next: float32 [8, 1024, 64], P('req', 'seq', 'cfg')
The draws below stay inside these ranges and needn't reach their ends.
Inputs may be any that keep to these rules, and one draw needn't show every extreme that they name: Text slot t of prompt p in branch c is live when t < text_len[c, p]; every draw has a length equal to 154.
All inputs are finite; a program needn't handle non-finite values.
Results may differ from the reference program's by a relative error of at most 0.02.
Values may be sent and summed in bfloat16 or wider, within the bound.
A program may use at most 128 MiB of HBM per device.

```python
import jax
import jax.numpy as jnp
from jax import lax

D = 1536
FF = 6144
HEAD = 64
PCH = 64
IMG = 1024
TXT = 192
TXT_MAX = 154
HEADS = 24
PROMPTS = 8


def draw_text_len(key, part):
    lengths = jax.random.randint(key, (2 * PROMPTS,), TXT_MAX // 4, TXT_MAX + 1)
    place = jax.random.randint(jax.random.fold_in(key, 7), (), 0, 2 * PROMPTS)
    lengths = jnp.where(jnp.arange(2 * PROMPTS) == place, TXT_MAX, lengths)
    return lengths.reshape(2, PROMPTS).astype(jnp.int32)


def projection_draw(key):
    base = jax.random.normal(key, (3, D, D), jnp.float32) * D ** (-0.5)
    return base


def draw_w_qkv_img(key, part):
    return projection_draw(jax.random.fold_in(key, 11)).astype(jnp.bfloat16)


def draw_w_qkv_txt(key, part):
    return projection_draw(jax.random.fold_in(key, 12)).astype(jnp.bfloat16)


def steps_of(key, shape, shards, low, high):
    def one(axis_at, blocks):
        draws = jax.random.uniform(jax.random.fold_in(jax.random.fold_in(key, 6), axis_at), (blocks,), jnp.float32, low / len(shards), high / len(shards))
        return jnp.repeat(jnp.exp(draws), shape[axis_at] // blocks).reshape((-1,) + (1,) * (len(shape) - axis_at - 1))

    level = one(*shards[0])
    for cut in shards[1:]:
        level = level * one(*cut)
    return level


def bell_draw(stream_key, dims, deviation, limit, cuts=(), held_as=jnp.bfloat16):
    factor_of = steps_of(stream_key, dims, cuts, -0.22, 0.18) if cuts else 1.0
    array = jax.random.normal(stream_key, dims, jnp.float32) * deviation * factor_of
    return jnp.minimum(jnp.maximum(array, -limit), limit).astype(held_as)


def setup_inputs(seed: int = 0) -> dict:
    arg_keys = jax.random.split(jax.random.key(seed), 13)
    img_state = bell_draw(arg_keys[0], (2, PROMPTS, IMG, D), 1.0, 6.0, ((0, 2), (1, 4), (2, 4)))
    txt_state = bell_draw(arg_keys[1], (2, PROMPTS, TXT, D), 1.0, 6.0, ((0, 2), (1, 4), (2, 4)))
    cond_vec = bell_draw(arg_keys[2], (2, PROMPTS, D), 1.0, 6.0, ((0, 2),), jnp.float32)
    text_len = draw_text_len(jax.random.fold_in(arg_keys[12], 71), 0)
    latent = bell_draw(arg_keys[4], (PROMPTS, IMG, PCH), 1.0, 6.0, ((0, 4), (1, 4), (2, 2)), jnp.float32)
    w_mod = bell_draw(arg_keys[5], (10 * D, D), D ** -0.5, 0.15625, ((0, 16),))
    w_qkv_img = draw_w_qkv_img(jax.random.fold_in(arg_keys[12], 71), 0)
    w_qkv_txt = draw_w_qkv_txt(jax.random.fold_in(arg_keys[12], 71), 0)
    w_attn_out = bell_draw(arg_keys[8], (D, D), 0.15, 2.0, ((0, 4),))
    w_up = bell_draw(arg_keys[9], (FF, D), D ** -0.5, 0.15625, ((0, 32),))
    w_down = bell_draw(arg_keys[10], (FF, D), FF ** -0.5, 0.078125, ((0, 32),))
    w_final = bell_draw(arg_keys[11], (D, PCH), 0.005, 0.078125)
    return {"img_state": img_state, "txt_state": txt_state, "cond_vec": cond_vec, "text_len": text_len, "latent": latent, "w_mod": w_mod, "w_qkv_img": w_qkv_img, "w_qkv_txt": w_qkv_txt, "w_attn_out": w_attn_out, "w_up": w_up, "w_down": w_down, "w_final": w_final}


def layer_norm(value):
    mean = lax.optimization_barrier(jnp.mean(value, axis=-1, keepdims=True))
    centered = value - mean
    spread = lax.optimization_barrier(jnp.mean(centered * centered, axis=-1, keepdims=True))
    return centered * lax.rsqrt(spread + 1e-06)

def one_stream(img, txt, mod, length, w_qkv_img, w_qkv_txt, w_attn_out, w_up, w_down, w_final):
    parts = mod.reshape(10, D)
    a_img = (layer_norm(img.astype(jnp.float32)) * (1.0 + parts[1]) + parts[0]).astype(jnp.bfloat16)
    a_txt = (layer_norm(txt.astype(jnp.float32)) * (1.0 + parts[7]) + parts[6]).astype(jnp.bfloat16)
    qkv_img = jnp.einsum('nd,jed->jne', a_img.astype(jnp.float32), w_qkv_img.astype(jnp.float32)).astype(jnp.bfloat16)
    qkv_txt = jnp.einsum('nd,jed->jne', a_txt.astype(jnp.float32), w_qkv_txt.astype(jnp.float32)).astype(jnp.bfloat16)
    query = qkv_img[0].reshape(IMG, HEADS, HEAD).astype(jnp.float32)
    keys = jnp.concatenate([qkv_img[1], qkv_txt[1]], axis=0).reshape(IMG + TXT, HEADS, HEAD).astype(jnp.float32)
    values = jnp.concatenate([qkv_img[2], qkv_txt[2]], axis=0).reshape(IMG + TXT, HEADS, HEAD).astype(jnp.float32)
    scores = jnp.einsum('qhe,khe->hqk', query, keys) * HEAD ** (-0.5)
    slots = jnp.arange(IMG + TXT)
    live = slots < IMG + length
    scores = jnp.where(live[None, None, :], scores, -1e+30)
    probs = jax.nn.softmax(scores, axis=-1).astype(jnp.bfloat16)
    attended = jnp.einsum('hqk,khe->qhe', probs.astype(jnp.float32), values).astype(jnp.bfloat16).reshape(IMG, D)
    proj = jnp.dot(attended, w_attn_out, preferred_element_type=jnp.float32)
    resid_one = (img.astype(jnp.float32) + parts[2] * proj).astype(jnp.bfloat16)
    normed = (layer_norm(resid_one.astype(jnp.float32)) * (1.0 + parts[4]) + parts[3]).astype(jnp.bfloat16)
    inner = lax.dot_general(normed, w_up, (((1,), (1,)), ((), ())), preferred_element_type=jnp.float32)
    hidden = jax.nn.gelu(inner, approximate=True).astype(jnp.bfloat16)
    mlp_out = jnp.dot(hidden, w_down, preferred_element_type=jnp.float32)
    resid_two = resid_one.astype(jnp.float32) + parts[5] * mlp_out
    final_in = (layer_norm(resid_two) * (1.0 + parts[9]) + parts[8]).astype(jnp.bfloat16)
    return jnp.dot(final_in, w_final, preferred_element_type=jnp.float32)

def reference(img_state, txt_state, cond_vec, text_len, latent, w_mod, w_qkv_img, w_qkv_txt, w_attn_out, w_up, w_down, w_final):
    cond_act = jax.nn.silu(cond_vec).astype(jnp.bfloat16)
    mod = jnp.einsum('cpd,ed->cpe', cond_act.astype(jnp.float32), w_mod.astype(jnp.float32))

    def run_item(item):
        return one_stream(item[0], item[1], item[2], item[3], w_qkv_img, w_qkv_txt, w_attn_out, w_up, w_down, w_final)
    items = (img_state.reshape(2 * PROMPTS, IMG, D), txt_state.reshape(2 * PROMPTS, TXT, D), mod.reshape(2 * PROMPTS, 10 * D), text_len.reshape(2 * PROMPTS))
    branch_vel = lax.map(run_item, items).reshape(2, PROMPTS, IMG, PCH)
    velocity = branch_vel[1] + 4.5 * (branch_vel[0] - branch_vel[1])
    latent_next = latent - 0.04 * velocity
    return (velocity, latent_next)
```

```python
import functools

import jax
import jax.numpy as jnp
from jax import lax
from jax.experimental import pallas as pl
from jax.experimental.pallas import tpu as pltpu
from jax.sharding import PartitionSpec as P

HEAD = 64
VMEM_BYTES = 56 * 1024 * 1024


def partner_2(shard, axis, apart):
    return lax.ppermute(shard, axis, [(i, i ^ 1 << apart) for i in range(lax.axis_size(axis))])


def layer_norm(value):
    mean = jnp.mean(value, axis=-1, keepdims=True)
    centered = value - mean
    spread = jnp.mean(centered * centered, axis=-1, keepdims=True)
    return centered * lax.rsqrt(spread + 1e-06)


def mlp_term(rows_in, up_block, down_block):
    inner = lax.dot_general(
        rows_in, up_block, (((1,), (1,)), ((), ())), preferred_element_type=jnp.float32
    )
    hidden = jax.nn.gelu(inner, approximate=True).astype(jnp.bfloat16)
    return jnp.dot(hidden, down_block, preferred_element_type=jnp.float32)


def local(
    img_state,
    txt_state,
    cond_vec,
    text_len,
    latent,
    w_mod,
    w_qkv_img,
    w_qkv_txt,
    w_attn_out,
    w_up,
    w_down,
    w_final,
):
    prompts_dev = img_state.shape[1]
    img_rows = img_state.shape[2]
    width = img_state.shape[3]
    cond_act = jax.nn.silu(cond_vec[0]).astype(jnp.bfloat16)
    mod_part = lax.dot_general(
        cond_act, w_mod, (((1,), (1,)), ((), ())), preferred_element_type=jnp.float32
    )
    mod_all = lax.all_gather(mod_part, ("req", "seq"), axis=1, tiled=True)
    mine = lax.dynamic_slice_in_dim(mod_all, lax.axis_index("req") * prompts_dev, prompts_dev, 0)
    parts = mine.reshape(prompts_dev, 10, 1, width)
    resid = img_state[0].astype(jnp.float32)
    a_img = (layer_norm(resid) * (1.0 + parts[:, 1]) + parts[:, 0]).astype(jnp.bfloat16)
    a_txt = (
        layer_norm(txt_state[0].astype(jnp.float32)) * (1.0 + parts[:, 7]) + parts[:, 6]
    ).astype(jnp.bfloat16)
    full_img, full_txt = (
        lax.all_gather(a_img, "seq", axis=1, tiled=True),
        lax.all_gather(a_txt, "seq", axis=1, tiled=True),
    )
    proj_img = jnp.einsum(
        "pnd,jed->jpne", full_img, w_qkv_img, preferred_element_type=jnp.float32
    ).astype(jnp.bfloat16)
    proj_txt = jnp.einsum(
        "pnd,jed->jpne", full_txt, w_qkv_txt, preferred_element_type=jnp.float32
    ).astype(jnp.bfloat16)
    total_img = full_img.shape[1]
    local_width = w_qkv_img.shape[1]
    heads_local = local_width // HEAD
    key_heads = jnp.concatenate([proj_img[1], proj_txt[1]], axis=1).reshape(
        prompts_dev, -1, heads_local, HEAD
    )
    value_heads = jnp.concatenate([proj_img[2], proj_txt[2]], axis=1).reshape(
        prompts_dev, -1, heads_local, HEAD
    )
    live = jnp.arange(key_heads.shape[1])[None, :] < (total_img + text_len[0])[:, None]
    block = min(512, total_img)
    queries = proj_img[0].reshape(prompts_dev, total_img // block, block, heads_local, HEAD)

    def attend(query):
        scores = jnp.einsum(
            "pqhe,pkhe->phqk", query, key_heads, preferred_element_type=jnp.float32
        ) * HEAD ** (-0.5)
        scores = jnp.where(live[:, None, None, :], scores, -1e30)
        probs = jax.nn.softmax(scores, axis=-1).astype(jnp.bfloat16)
        return jnp.einsum(
            "phqk,pkhe->pqhe", probs, value_heads, preferred_element_type=jnp.float32
        ).astype(jnp.bfloat16)

    attended = lax.map(attend, jnp.moveaxis(queries, 1, 0))
    attended = jnp.moveaxis(attended, 0, 1).reshape(prompts_dev, total_img, local_width)
    proj = jnp.swapaxes(
        lax.psum_scatter(
            jnp.einsum(
                "pnh,hd->npd", attended, w_attn_out, preferred_element_type=jnp.float32
            ).astype(jnp.bfloat16),
            "seq",
            scatter_dimension=0,
            tiled=True,
        ).astype(jnp.float32),
        0,
        1,
    )
    resid_one = (resid + parts[:, 2] * proj).astype(jnp.bfloat16)
    normed = (layer_norm(resid_one.astype(jnp.float32)) * (1.0 + parts[:, 4]) + parts[:, 3]).astype(
        jnp.bfloat16
    )
    own_rows = normed.reshape(prompts_dev * img_rows, width)
    both = lax.all_gather(own_rows, "cfg", axis=0, tiled=True)
    partial_out = mlp_term(
        both,
        lax.all_gather(w_up, ("req", "seq"), axis=0, tiled=True),
        lax.all_gather(w_down, ("req", "seq"), axis=0, tiled=True),
    )
    mlp_out = lax.psum_scatter(
        partial_out.astype(jnp.bfloat16), "cfg", scatter_dimension=0, tiled=True
    ).astype(jnp.float32)
    mlp_out = mlp_out.reshape(prompts_dev, img_rows, width)
    resid_two = resid_one.astype(jnp.float32) + parts[:, 5] * mlp_out
    final_in = (layer_norm(resid_two) * (1.0 + parts[:, 9]) + parts[:, 8]).astype(jnp.bfloat16)
    branch_vel = jnp.einsum("pnd,dc->pnc", final_in, w_final, preferred_element_type=jnp.float32)
    return guide(branch_vel, latent)

def flip(shard, bits):
    size = lax.axis_size("seq")
    return lax.ppermute(shard, "seq", [(i, i ^ bits) for i in range(size)])


def norm_rows(rows, scale, shift):
    return (layer_norm(rows.astype(jnp.float32)) * (1.0 + scale) + shift).astype(jnp.bfloat16)


def across(left, right):
    return lax.dot_general(
        left, right, (((1,), (1,)), ((), ())), preferred_element_type=jnp.float32
    )


def qkv_kernel(owners, img_rows, txt_rows, *refs):
    count = len(owners)
    pieces = refs[:count]
    mod, w_img, w_txt, img_out, txt_out, txt_in = refs[count:]
    for at, (piece, owner) in enumerate(zip(pieces, owners)):
        img = norm_rows(piece[:img_rows], mod[owner, 1:2], mod[owner, 0:1])
        img_out[pl.ds(at * img_rows, img_rows)] = across(img, w_img[...]).astype(jnp.bfloat16)
        txt_in[pl.ds(at * txt_rows, txt_rows)] = norm_rows(
            piece[img_rows:], mod[owner, 7:8], mod[owner, 6:7]
        )
    txt_out[...] = across(txt_in[...], w_txt[...]).astype(jnp.bfloat16)


def project(pieces, owners, img_rows, parts, w_img, w_txt):
    count = len(pieces)
    txt_rows = pieces[0].shape[0] - img_rows
    width = pieces[0].shape[1]
    out = w_img.shape[0]
    rows = count * (img_rows + txt_rows)
    return pl.pallas_call(
        functools.partial(qkv_kernel, owners, img_rows, txt_rows),
        out_shape=(
            jax.ShapeDtypeStruct((count * img_rows, out), jnp.bfloat16),
            jax.ShapeDtypeStruct((count * txt_rows, out), jnp.bfloat16),
        ),
        in_specs=[pl.BlockSpec(memory_space=pltpu.VMEM)] * (count + 3),
        out_specs=(pl.BlockSpec(memory_space=pltpu.VMEM),) * 2,
        scratch_shapes=[pltpu.VMEM((count * txt_rows, width), jnp.bfloat16)],
        compiler_params=pltpu.CompilerParams(vmem_limit_bytes=VMEM_BYTES),
        cost_estimate=pl.CostEstimate(
            flops=2 * rows * width * out, bytes_accessed=4 * out * width, transcendentals=0
        ),
    )(*pieces, parts, w_img, w_txt)


def attend_kernel(
    txt_rows, prompt, length, starts, qa, qb, ka, kb, va, vb, tka, tkb, tva, tvb, out
):
    first = lax.broadcasted_iota(jnp.int32, (1, 2 * HEAD), 1) < HEAD
    column = lax.broadcasted_iota(jnp.int32, (1, 2 * txt_rows), 1)
    live = []
    for base in (0, 2):
        slot = jnp.where(
            column < txt_rows, starts[base] + column, starts[base + 1] + column - txt_rows
        )
        live.append(slot < length[prompt])
    keys = (ka[...], kb[...], tka[...], tkb[...])
    values = (va[...], vb[...], tva[...], tvb[...])
    one = jnp.ones((), jnp.bfloat16)
    zero = jnp.zeros((), jnp.bfloat16)
    held = [
        [jnp.where(first, value, one) for value in values],
        [jnp.where(first, one, value) for value in values],
    ]
    for side, q_ref in enumerate((qa, qb)):
        query = q_ref[...] * jnp.asarray(HEAD ** (-0.5), jnp.bfloat16)
        sums = []
        for head in range(2):
            masked = jnp.where(first, query, zero) if head == 0 else jnp.where(first, zero, query)
            scores = [across(masked, key) for key in keys]
            for text in range(2):
                scores[2 + text] = jnp.where(live[text], scores[2 + text], -1e30)
            top = functools.reduce(
                jnp.maximum, [jnp.max(score, axis=-1, keepdims=True) for score in scores]
            )
            total = None
            for score, value in zip(scores, held[head]):
                weight = jnp.exp(score - top).astype(jnp.bfloat16)
                term = jnp.dot(weight, value, preferred_element_type=jnp.float32)
                total = term if total is None else total + term
            sums.append(total)
        out[side] = jnp.where(
            first, sums[0] / sums[0][:, HEAD : HEAD + 1], sums[1] / sums[1][:, 0:1]
        ).astype(jnp.bfloat16)


def attention(prompt, length, starts, near, far, img_rows):
    img_near, txt_near = near
    img_far, txt_far = far
    lanes = 2 * HEAD
    pairs = img_near.shape[1] // (3 * lanes)
    txt_rows = txt_far.shape[0] // 2
    half = 2 * img_rows
    smem = pl.BlockSpec(memory_space=pltpu.SMEM)

    def spec(rows, row_of, third):
        return pl.BlockSpec((rows, lanes), lambda j, i: (row_of(i), third * pairs + j))

    specs = [smem, smem]
    specs += [spec(img_rows, lambda i: 2 * prompt + i, 0), spec(img_rows, lambda i: i, 0)]
    for third in (1, 2):
        specs += [spec(half, lambda i: prompt, third), spec(half, lambda i: 0, third)]
    for third in (1, 2):
        specs += [
            spec(2 * txt_rows, lambda i: prompt, third),
            spec(2 * txt_rows, lambda i: 0, third),
        ]
    keys = 2 * half + 4 * txt_rows
    out = pl.pallas_call(
        functools.partial(attend_kernel, txt_rows, prompt),
        grid=(pairs, 2),
        out_shape=jax.ShapeDtypeStruct((2, half, pairs * lanes), jnp.bfloat16),
        in_specs=specs,
        out_specs=pl.BlockSpec((2, img_rows, lanes), lambda j, i: (0, i, j)),
        compiler_params=pltpu.CompilerParams(vmem_limit_bytes=VMEM_BYTES),
        cost_estimate=pl.CostEstimate(
            flops=16 * 2 * half * keys * pairs * lanes,
            bytes_accessed=8 * half * pairs * lanes,
            transcendentals=2 * half * keys * pairs * 2,
        ),
    )(
        length, starts,
        img_near, img_far, img_near, img_far, img_near, img_far,
        txt_near, txt_far, txt_near, txt_far,
    )
    return out.reshape(2 * half, pairs * lanes)


def tail_kernel(prompt, img_rows, *refs):
    heads, outs, pieces = refs[0:4], refs[4:8], refs[8:12]
    mod, up, down, keep, send, resid_out, state = refs[12:]
    step = pl.program_id(0)
    block = 2 * lax.rem(step, 2) + (1 - step // 2)
    for at in range(4):

        @pl.when(block == at)
        def _():
            state[...] = pieces[at][:img_rows]

    proj = None
    for head, weight in zip(heads, outs):
        term = jnp.dot(head[...], weight[...], preferred_element_type=jnp.float32)
        proj = term if proj is None else proj + term
    resid = (state[...].astype(jnp.float32) + mod[prompt, 2:3] * proj).astype(jnp.bfloat16)

    @pl.when(block == 0)
    def _():
        resid_out[...] = resid

    normed = norm_rows(resid, mod[prompt, 4:5], mod[prompt, 3:4])
    hidden_units = up.shape[0]
    cut = 512
    total = None
    for start in range(0, hidden_units, cut):
        inner = across(normed, up[pl.ds(start, cut)])
        hidden = jax.nn.gelu(inner, approximate=True).astype(jnp.bfloat16)
        term = jnp.dot(hidden, down[pl.ds(start, cut)], preferred_element_type=jnp.float32)
        total = term if total is None else total + term
    total = total.astype(jnp.bfloat16)

    @pl.when(step < 2)
    def _():
        send[...] = total

    @pl.when(step >= 2)
    def _():
        keep[...] = total


def tail(prompt, heads, outs, pieces, parts, up, down, img_rows):
    width = up.shape[1]
    local_width = heads[0].shape[1]

    def block_of(step):
        return 2 * lax.rem(step, 2) + (1 - step // 2)

    def spec(flipped):
        return pl.BlockSpec((img_rows, local_width), lambda t: (block_of(t) ^ flipped, 0))

    vmem = pl.BlockSpec(memory_space=pltpu.VMEM)
    rows = 4 * img_rows
    return pl.pallas_call(
        functools.partial(tail_kernel, prompt, img_rows),
        grid=(4,),
        out_shape=(
            jax.ShapeDtypeStruct((2 * img_rows, width), jnp.bfloat16),
            jax.ShapeDtypeStruct((2 * img_rows, width), jnp.bfloat16),
            jax.ShapeDtypeStruct((img_rows, width), jnp.bfloat16),
        ),
        in_specs=[spec(r) for r in range(4)] + [vmem] * 11,
        out_specs=(
            pl.BlockSpec((img_rows, width), lambda t: (jnp.maximum(t - 2, 0), 0)),
            pl.BlockSpec((img_rows, width), lambda t: (jnp.minimum(t, 1), 0)),
            pl.BlockSpec((img_rows, width), lambda t: (0, 0)),
        ),
        scratch_shapes=[pltpu.VMEM((img_rows, width), jnp.bfloat16)],
        compiler_params=pltpu.CompilerParams(vmem_limit_bytes=VMEM_BYTES),
        cost_estimate=pl.CostEstimate(
            flops=2 * rows * width * (width + 2 * up.shape[0]),
            bytes_accessed=2 * width * (width + 2 * up.shape[0]) + 8 * rows * width,
            transcendentals=rows * up.shape[0],
        ),
    )(*heads, *outs, *pieces, parts, up, down)


def final_kernel(prompts, img_rows, *refs):
    mod, w_final, out = refs[4 * prompts :]
    for prompt in range(prompts):
        resid, keep, core, chip = refs[4 * prompt : 4 * prompt + 4]
        mlp = (
            keep[:img_rows].astype(jnp.float32)
            + core[:img_rows].astype(jnp.float32)
            + chip[...].astype(jnp.float32)
        )
        two = resid[...].astype(jnp.float32) + mod[prompt, 5:6] * mlp
        last = (layer_norm(two) * (1.0 + mod[prompt, 9:10]) + mod[prompt, 8:9]).astype(
            jnp.bfloat16
        )
        out[prompt] = jnp.dot(last, w_final[...], preferred_element_type=jnp.float32)


def fast(
    img_state,
    txt_state,
    cond_vec,
    text_len,
    latent,
    w_mod,
    w_qkv_img,
    w_qkv_txt,
    w_attn_out,
    w_up,
    w_down,
    w_final,
):
    prompts = img_state.shape[1]
    img_rows = img_state.shape[2]
    txt_rows = txt_state.shape[2]
    width = img_state.shape[3]
    own = [jnp.concatenate([img_state[0, p], txt_state[0, p]], axis=0) for p in range(prompts)]
    pieces = [[rows, flip(rows, 1), flip(rows, 2)] for rows in own]
    for rows in pieces:
        rows.append(flip(rows[2], 1))
    up = lax.all_gather(w_up, ("cfg", "req"), axis=0, tiled=True)
    down = lax.all_gather(w_down, ("cfg", "req"), axis=0, tiled=True)
    cond_act = jax.nn.silu(cond_vec[0]).astype(jnp.bfloat16)
    mod_part = across(cond_act, w_mod)
    mod_all = lax.all_gather(mod_part, ("req", "seq"), axis=1, tiled=True)
    mine = lax.dynamic_slice_in_dim(mod_all, lax.axis_index("req") * prompts, prompts, 0)
    parts = mine.reshape(prompts, 10, width)
    w_img = w_qkv_img.reshape(-1, width)
    w_txt = w_qkv_txt.reshape(-1, width)
    me = lax.axis_index("seq")
    starts = jnp.stack([txt_rows * (me ^ r) for r in range(4)]).astype(jnp.int32)
    near = project(
        [rows[r] for rows in pieces for r in (0, 1)],
        [p for p in range(prompts) for r in (0, 1)],
        img_rows, parts, w_img, w_txt,
    )
    outs = [w_attn_out, flip(w_attn_out, 1), flip(w_attn_out, 2)]
    outs.append(flip(outs[2], 1))
    results = []
    for p in range(prompts):
        far = project(pieces[p][2:], [p, p], img_rows, parts, w_img, w_txt)
        own_heads = attention(p, text_len[0], starts, near, far, img_rows)
        heads = [own_heads, flip(own_heads, 1), flip(own_heads, 2)]
        heads.append(flip(heads[2], 1))
        keep, send, resid = tail(p, heads, outs, pieces[p], parts, up, down, img_rows)
        core = flip(send, 1)
        chip = flip(
            (keep[img_rows:].astype(jnp.float32) + core[img_rows:].astype(jnp.float32)).astype(
                jnp.bfloat16
            ),
            2,
        )
        results += [resid, keep, core, chip]
    vmem = pl.BlockSpec(memory_space=pltpu.VMEM)
    branch_vel = pl.pallas_call(
        functools.partial(final_kernel, prompts, img_rows),
        out_shape=jax.ShapeDtypeStruct((prompts, img_rows, w_final.shape[1]), jnp.float32),
        in_specs=[vmem] * (4 * prompts + 2),
        out_specs=vmem,
        compiler_params=pltpu.CompilerParams(vmem_limit_bytes=VMEM_BYTES),
    )(*results, parts, w_final)
    return guide(branch_vel, latent)


def guide(branch_vel, latent):
    half_width = latent.shape[2]
    branch_index = lax.axis_index("cfg")
    own_half = lax.dynamic_slice_in_dim(branch_vel, branch_index * half_width, half_width, 2)
    other_half = lax.dynamic_slice_in_dim(
        branch_vel, (1 - branch_index) * half_width, half_width, 2
    )
    partner = partner_2(other_half.astype(jnp.bfloat16), "cfg", 0).astype(other_half.dtype)
    first = branch_index == 0
    cond_vel = jnp.where(first, own_half, partner)
    uncond_vel = jnp.where(first, partner, own_half)
    velocity = uncond_vel + 4.5 * (cond_vel - uncond_vel)
    latent_next = latent - 0.04 * velocity
    return (velocity, latent_next)


def plan(*shards):
    img_state, txt_state, w_qkv_img = shards[0], shards[1], shards[6]
    fits = (
        lax.axis_size("seq") == 4
        and img_state.shape[2] % 128 == 0
        and txt_state.shape[2] % 16 == 0
        and w_qkv_img.shape[1] % (2 * HEAD) == 0
    )
    return fast(*shards) if fits else local(*shards)


def solution(mesh):
    placed = (
        P("cfg", "req", "seq", None),
        P("cfg", "req", "seq", None),
        P("cfg", None, None),
        P("cfg", "req"),
        P("req", "seq", "cfg"),
        P(("req", "seq"), None),
        P(None, "seq", None),
        P(None, "seq", None),
        P("seq", None),
        P(("cfg", "req", "seq"), None),
        P(("cfg", "req", "seq"), None),
        P(),
    )
    return jax.shard_map(
        plan,
        mesh=mesh,
        in_specs=placed,
        out_specs=(P("req", "seq", "cfg"), P("req", "seq", "cfg")),
        check_vma=False,
    )
```

```python
import functools

import jax
import jax.numpy as jnp
from jax import lax
from jax.experimental import pallas as pl
from jax.experimental.pallas import tpu as pltpu
from jax.sharding import PartitionSpec as P

HEAD = 64
VMEM_BYTES = 56 * 1024 * 1024


def partner_2(shard, axis, apart):
    return lax.ppermute(shard, axis, [(i, i ^ 1 << apart) for i in range(lax.axis_size(axis))])


def layer_norm(value):
    mean = jnp.mean(value, axis=-1, keepdims=True)
    centered = value - mean
    spread = jnp.mean(centered * centered, axis=-1, keepdims=True)
    return centered * lax.rsqrt(spread + 1e-06)


def mlp_term(rows_in, up_block, down_block):
    inner = lax.dot_general(
        rows_in, up_block, (((1,), (1,)), ((), ())), preferred_element_type=jnp.float32
    )
    hidden = jax.nn.gelu(inner, approximate=True).astype(jnp.bfloat16)
    return jnp.dot(hidden, down_block, preferred_element_type=jnp.float32)


def local(
    img_state,
    txt_state,
    cond_vec,
    text_len,
    latent,
    w_mod,
    w_qkv_img,
    w_qkv_txt,
    w_attn_out,
    w_up,
    w_down,
    w_final,
):
    prompts_dev = img_state.shape[1]
    img_rows = img_state.shape[2]
    width = img_state.shape[3]
    cond_act = jax.nn.silu(cond_vec[0]).astype(jnp.bfloat16)
    mod_part = lax.dot_general(
        cond_act, w_mod, (((1,), (1,)), ((), ())), preferred_element_type=jnp.float32
    )
    mod_all = lax.all_gather(mod_part, ("req", "seq"), axis=1, tiled=True)
    mine = lax.dynamic_slice_in_dim(mod_all, lax.axis_index("req") * prompts_dev, prompts_dev, 0)
    parts = mine.reshape(prompts_dev, 10, 1, width)
    resid = img_state[0].astype(jnp.float32)
    a_img = (layer_norm(resid) * (1.0 + parts[:, 1]) + parts[:, 0]).astype(jnp.bfloat16)
    a_txt = (
        layer_norm(txt_state[0].astype(jnp.float32)) * (1.0 + parts[:, 7]) + parts[:, 6]
    ).astype(jnp.bfloat16)
    full_img, full_txt = (
        lax.all_gather(a_img, "seq", axis=1, tiled=True),
        lax.all_gather(a_txt, "seq", axis=1, tiled=True),
    )
    proj_img = jnp.einsum(
        "pnd,jed->jpne", full_img, w_qkv_img, preferred_element_type=jnp.float32
    ).astype(jnp.bfloat16)
    proj_txt = jnp.einsum(
        "pnd,jed->jpne", full_txt, w_qkv_txt, preferred_element_type=jnp.float32
    ).astype(jnp.bfloat16)
    total_img = full_img.shape[1]
    local_width = w_qkv_img.shape[1]
    heads_local = local_width // HEAD
    key_heads = jnp.concatenate([proj_img[1], proj_txt[1]], axis=1).reshape(
        prompts_dev, -1, heads_local, HEAD
    )
    value_heads = jnp.concatenate([proj_img[2], proj_txt[2]], axis=1).reshape(
        prompts_dev, -1, heads_local, HEAD
    )
    live = jnp.arange(key_heads.shape[1])[None, :] < (total_img + text_len[0])[:, None]
    block = min(512, total_img)
    queries = proj_img[0].reshape(prompts_dev, total_img // block, block, heads_local, HEAD)

    def attend(query):
        scores = jnp.einsum(
            "pqhe,pkhe->phqk", query, key_heads, preferred_element_type=jnp.float32
        ) * HEAD ** (-0.5)
        scores = jnp.where(live[:, None, None, :], scores, -1e30)
        probs = jax.nn.softmax(scores, axis=-1).astype(jnp.bfloat16)
        return jnp.einsum(
            "phqk,pkhe->pqhe", probs, value_heads, preferred_element_type=jnp.float32
        ).astype(jnp.bfloat16)

    attended = lax.map(attend, jnp.moveaxis(queries, 1, 0))
    attended = jnp.moveaxis(attended, 0, 1).reshape(prompts_dev, total_img, local_width)
    proj = jnp.swapaxes(
        lax.psum_scatter(
            jnp.einsum(
                "pnh,hd->npd", attended, w_attn_out, preferred_element_type=jnp.float32
            ).astype(jnp.bfloat16),
            "seq",
            scatter_dimension=0,
            tiled=True,
        ).astype(jnp.float32),
        0,
        1,
    )
    resid_one = (resid + parts[:, 2] * proj).astype(jnp.bfloat16)
    normed = (layer_norm(resid_one.astype(jnp.float32)) * (1.0 + parts[:, 4]) + parts[:, 3]).astype(
        jnp.bfloat16
    )
    own_rows = normed.reshape(prompts_dev * img_rows, width)
    both = lax.all_gather(own_rows, "cfg", axis=0, tiled=True)
    partial_out = mlp_term(
        both,
        lax.all_gather(w_up, ("req", "seq"), axis=0, tiled=True),
        lax.all_gather(w_down, ("req", "seq"), axis=0, tiled=True),
    )
    mlp_out = lax.psum_scatter(
        partial_out.astype(jnp.bfloat16), "cfg", scatter_dimension=0, tiled=True
    ).astype(jnp.float32)
    mlp_out = mlp_out.reshape(prompts_dev, img_rows, width)
    resid_two = resid_one.astype(jnp.float32) + parts[:, 5] * mlp_out
    final_in = (layer_norm(resid_two) * (1.0 + parts[:, 9]) + parts[:, 8]).astype(jnp.bfloat16)
    branch_vel = jnp.einsum("pnd,dc->pnc", final_in, w_final, preferred_element_type=jnp.float32)
    return guide(branch_vel, latent)

def flip(shard, bits, axis="seq"):
    return lax.ppermute(shard, axis, [(i, i ^ bits) for i in range(lax.axis_size(axis))])


def after(value, first):
    return lax.optimization_barrier((value, first))[0]


def norm_rows(rows, scale, shift):
    return (layer_norm(rows.astype(jnp.float32)) * (1.0 + scale) + shift).astype(jnp.bfloat16)


def across(left, right):
    return lax.dot_general(
        left, right, (((1,), (1,)), ((), ())), preferred_element_type=jnp.float32
    )


def mod_kernel(cond, weight, out, part, got, send_sem, recv_sem):
    reqs, seqs = lax.axis_size("req"), lax.axis_size("seq")
    group = reqs * seqs
    cfg, req = lax.axis_index("cfg"), lax.axis_index("req")
    me = req * seqs + lax.axis_index("seq")
    prompts = part.shape[1]
    barrier = pltpu.get_barrier_semaphore()
    for apart in range(1, group):
        peer = lax.rem(me + apart, group)
        pl.semaphore_signal(
            barrier,
            inc=1,
            device_id=(cfg, peer // seqs, lax.rem(peer, seqs)),
            device_id_type=pl.DeviceIdType.MESH,
        )
    rows = across(jax.nn.silu(cond[...]).astype(jnp.bfloat16), weight[...])
    for at in range(reqs):
        part[at] = rows[at * prompts : (at + 1) * prompts]
    pl.semaphore_wait(barrier, group - 1)
    copies = []
    for apart in range(1, group):
        peer = lax.rem(me + apart, group)
        copy = pltpu.make_async_remote_copy(
            src_ref=part.at[peer // seqs],
            dst_ref=got.at[me],
            send_sem=send_sem.at[apart],
            recv_sem=recv_sem.at[apart],
            device_id=(cfg, peer // seqs, lax.rem(peer, seqs)),
            device_id_type=pl.DeviceIdType.MESH,
        )
        copy.start()
        copies.append(copy)
    got[me] = part[req]
    for copy in copies:
        copy.wait()
    out[...] = got[...]


def modulation(cond, weight):
    reqs, seqs = lax.axis_size("req"), lax.axis_size("seq")
    group, prompts, columns = reqs * seqs, cond.shape[0] // reqs, weight.shape[0]
    vmem = pl.BlockSpec(memory_space=pltpu.VMEM)
    got = pl.pallas_call(
        mod_kernel,
        out_shape=jax.ShapeDtypeStruct((group, prompts, columns), jnp.float32),
        in_specs=[vmem, vmem],
        out_specs=vmem,
        scratch_shapes=[
            pltpu.VMEM((reqs, prompts, columns), jnp.float32),
            pltpu.VMEM((group, prompts, columns), jnp.float32),
            pltpu.SemaphoreType.DMA((group,)),
            pltpu.SemaphoreType.DMA((group,)),
        ],
        compiler_params=pltpu.CompilerParams(
            collective_id=0, has_side_effects=True, vmem_limit_bytes=VMEM_BYTES
        ),
        cost_estimate=pl.CostEstimate(
            flops=2 * cond.size * columns, bytes_accessed=2 * weight.size, transcendentals=0
        ),
    )(cond, weight)
    return jnp.swapaxes(got, 0, 1).reshape(prompts, 10, -1)


def qkv_kernel(owners, img_rows, txt_rows, *refs):
    count = len(owners)
    pieces = refs[:count]
    mod, w_img, w_txt, img_out, txt_out, txt_in = refs[count:]
    for at, (piece, owner) in enumerate(zip(pieces, owners)):
        img = norm_rows(piece[:img_rows], mod[owner, 1:2], mod[owner, 0:1])
        img_out[pl.ds(at * img_rows, img_rows)] = across(img, w_img[...]).astype(jnp.bfloat16)
        txt_in[pl.ds(at * txt_rows, txt_rows)] = norm_rows(
            piece[img_rows:], mod[owner, 7:8], mod[owner, 6:7]
        )
    txt_out[...] = across(txt_in[...], w_txt[...]).astype(jnp.bfloat16)


def project(pieces, owners, img_rows, parts, w_img, w_txt):
    count = len(pieces)
    txt_rows = pieces[0].shape[0] - img_rows
    width = pieces[0].shape[1]
    out = w_img.shape[0]
    rows = count * (img_rows + txt_rows)
    return pl.pallas_call(
        functools.partial(qkv_kernel, owners, img_rows, txt_rows),
        out_shape=(
            jax.ShapeDtypeStruct((count * img_rows, out), jnp.bfloat16),
            jax.ShapeDtypeStruct((count * txt_rows, out), jnp.bfloat16),
        ),
        in_specs=[pl.BlockSpec(memory_space=pltpu.VMEM)] * (count + 3),
        out_specs=(pl.BlockSpec(memory_space=pltpu.VMEM),) * 2,
        scratch_shapes=[pltpu.VMEM((count * txt_rows, width), jnp.bfloat16)],
        compiler_params=pltpu.CompilerParams(vmem_limit_bytes=VMEM_BYTES),
        cost_estimate=pl.CostEstimate(
            flops=2 * rows * width * out, bytes_accessed=4 * out * width, transcendentals=0
        ),
    )(*pieces, parts, w_img, w_txt)


def attend_kernel(
    txt_rows, prompt, length, starts, qa, qb, ka, kb, va, vb, tka, tkb, tva, tvb, out
):
    first = lax.broadcasted_iota(jnp.int32, (1, 2 * HEAD), 1) < HEAD
    column = lax.broadcasted_iota(jnp.int32, (1, 2 * txt_rows), 1)
    live = []
    for base in (0, 2):
        slot = jnp.where(
            column < txt_rows, starts[base] + column, starts[base + 1] + column - txt_rows
        )
        live.append(slot < length[prompt])
    keys = (ka[...], kb[...], tka[...], tkb[...])
    values = (va[...], vb[...], tva[...], tvb[...])
    one = jnp.ones((), jnp.bfloat16)
    zero = jnp.zeros((), jnp.bfloat16)
    held = [
        [jnp.where(first, value, one) for value in values],
        [jnp.where(first, one, value) for value in values],
    ]
    for side, q_ref in enumerate((qa, qb)):
        query = q_ref[...] * jnp.asarray(HEAD ** (-0.5), jnp.bfloat16)
        sums = []
        for head in range(2):
            masked = jnp.where(first, query, zero) if head == 0 else jnp.where(first, zero, query)
            scores = [across(masked, key) for key in keys]
            for text in range(2):
                scores[2 + text] = jnp.where(live[text], scores[2 + text], -1e30)
            top = functools.reduce(
                jnp.maximum, [jnp.max(score, axis=-1, keepdims=True) for score in scores]
            )
            total = None
            for score, value in zip(scores, held[head]):
                weight = jnp.exp(score - top).astype(jnp.bfloat16)
                term = jnp.dot(weight, value, preferred_element_type=jnp.float32)
                total = term if total is None else total + term
            sums.append(total)
        out[0, side] = jnp.where(
            first, sums[0] / sums[0][:, HEAD : HEAD + 1], sums[1] / sums[1][:, 0:1]
        ).astype(jnp.bfloat16)


def attention(prompt, length, starts, near, far, img_rows):
    img_near, txt_near = near
    img_far, txt_far = far
    lanes = 2 * HEAD
    pairs = img_near.shape[1] // (3 * lanes)
    txt_rows = txt_far.shape[0] // 2
    half = 2 * img_rows
    smem = pl.BlockSpec(memory_space=pltpu.SMEM)

    def spec(rows, row_of, third):
        return pl.BlockSpec((rows, lanes), lambda j, i: (row_of(i), third * pairs + j))

    specs = [smem, smem]
    specs += [spec(img_rows, lambda i: 2 * prompt + i, 0), spec(img_rows, lambda i: i, 0)]
    for third in (1, 2):
        specs += [spec(half, lambda i: prompt, third), spec(half, lambda i: 0, third)]
    for third in (1, 2):
        specs += [
            spec(2 * txt_rows, lambda i: prompt, third),
            spec(2 * txt_rows, lambda i: 0, third),
        ]
    keys = 2 * half + 4 * txt_rows
    out = pl.pallas_call(
        functools.partial(attend_kernel, txt_rows, prompt),
        grid=(pairs, 2),
        out_shape=jax.ShapeDtypeStruct((2, 2, img_rows, pairs * lanes), jnp.bfloat16),
        in_specs=specs,
        out_specs=pl.BlockSpec((1, 2, img_rows, lanes), lambda j, i: (i, 0, 0, j)),
        compiler_params=pltpu.CompilerParams(vmem_limit_bytes=VMEM_BYTES),
        cost_estimate=pl.CostEstimate(
            flops=16 * 2 * half * keys * pairs * lanes,
            bytes_accessed=8 * half * pairs * lanes,
            transcendentals=2 * half * keys * pairs * 2,
        ),
    )(
        length, starts,
        img_near, img_far, img_near, img_far, img_near, img_far,
        txt_near, txt_far, txt_near, txt_far,
    )
    return out.reshape(2 * half, pairs * lanes)


def tail_kernel(prompt, img_rows, *refs):
    heads, outs, pieces, shards = refs[0:4], refs[4:8], refs[8:12], refs[12:20]
    mod, keep, send, resid_out, state, up, down, sems = refs[20:]
    step = pl.program_id(0)
    units = shards[0].shape[0] // 2
    copies = []
    for at, shard in enumerate(shards):
        for which, target in enumerate((up, down)):
            copies.append(
                pltpu.make_async_copy(
                    shard.at[pl.ds(which * units, units)],
                    target.at[pl.ds(at * units, units)],
                    sems.at[2 * at + which],
                )
            )

    @pl.when(step == 0)
    def _():
        for copy in copies:
            copy.start()
        state[:img_rows] = pieces[1][:img_rows]
        state[img_rows:] = pieces[3][:img_rows]

    @pl.when(step == 1)
    def _():
        state[:img_rows] = pieces[0][:img_rows]
        state[img_rows:] = pieces[2][:img_rows]

    proj = None
    for at in range(4):
        rows = heads[at][...]
        if at >= 2:
            rows = jnp.concatenate([rows[img_rows:], rows[:img_rows]], axis=0)
        term = jnp.dot(rows, outs[at][...], preferred_element_type=jnp.float32)
        proj = term if proj is None else proj + term
    resid = (state[...].astype(jnp.float32) + mod[prompt, 2:3] * proj).astype(jnp.bfloat16)

    normed = norm_rows(resid, mod[prompt, 4:5], mod[prompt, 3:4])

    @pl.when(step == 0)
    def _():
        for copy in copies:
            copy.wait()

    cut = 512
    total = None
    for start in range(0, up.shape[0], cut):
        inner = across(normed, up[pl.ds(start, cut)])
        hidden = jax.nn.gelu(inner, approximate=True).astype(jnp.bfloat16)
        term = jnp.dot(hidden, down[pl.ds(start, cut)], preferred_element_type=jnp.float32)
        total = term if total is None else total + term
    total = total.astype(jnp.bfloat16)

    @pl.when(step == 0)
    def _():
        send[...] = total

    @pl.when(step == 1)
    def _():
        keep[...] = total
        resid_out[...] = resid[:img_rows]


def tail(prompt, heads, outs, pieces, parts, shards, img_rows):
    width = parts.shape[2]
    local_width = heads[0].shape[1]
    units = shards[0].shape[0] // 2 * len(shards)

    def spec(apart):
        return pl.BlockSpec((2 * img_rows, local_width), lambda t: ((1 - t) ^ (apart % 2), 0))

    vmem = pl.BlockSpec(memory_space=pltpu.VMEM)
    rows = 4 * img_rows
    return pl.pallas_call(
        functools.partial(tail_kernel, prompt, img_rows),
        grid=(2,),
        out_shape=(
            jax.ShapeDtypeStruct((2 * img_rows, width), jnp.bfloat16),
            jax.ShapeDtypeStruct((2 * img_rows, width), jnp.bfloat16),
            jax.ShapeDtypeStruct((img_rows, width), jnp.bfloat16),
        ),
        in_specs=[spec(r) for r in range(4)]
        + [vmem] * 8
        + [pl.BlockSpec(memory_space=pl.ANY)] * len(shards)
        + [vmem],
        out_specs=(
            pl.BlockSpec((2 * img_rows, width), lambda t: (0, 0)),
            pl.BlockSpec((2 * img_rows, width), lambda t: (0, 0)),
            pl.BlockSpec((img_rows, width), lambda t: (0, 0)),
        ),
        scratch_shapes=[
            pltpu.VMEM((2 * img_rows, width), jnp.bfloat16),
            pltpu.VMEM((units, width), jnp.bfloat16),
            pltpu.VMEM((units, width), jnp.bfloat16),
            pltpu.SemaphoreType.DMA((2 * len(shards),)),
        ],
        compiler_params=pltpu.CompilerParams(vmem_limit_bytes=VMEM_BYTES),
        cost_estimate=pl.CostEstimate(
            flops=2 * rows * width * (width + 2 * units),
            bytes_accessed=2 * width * (width + 2 * units) + 8 * rows * width,
            transcendentals=rows * units,
        ),
    )(*heads, *outs, *pieces, *shards, parts)


def final_kernel(prompts, img_rows, *refs):
    mod, w_final, out = refs[4 * prompts :]
    for prompt in range(prompts):
        resid, keep, core, chip = refs[4 * prompt : 4 * prompt + 4]
        mlp = (
            keep[:img_rows].astype(jnp.float32)
            + core[:img_rows].astype(jnp.float32)
            + chip[...].astype(jnp.float32)
        )
        two = resid[...].astype(jnp.float32) + mod[prompt, 5:6] * mlp
        last = (layer_norm(two) * (1.0 + mod[prompt, 9:10]) + mod[prompt, 8:9]).astype(
            jnp.bfloat16
        )
        out[prompt] = jnp.dot(last, w_final[...], preferred_element_type=jnp.float32)


def fast(
    img_state,
    txt_state,
    cond_vec,
    text_len,
    latent,
    w_mod,
    w_qkv_img,
    w_qkv_txt,
    w_attn_out,
    w_up,
    w_down,
    w_final,
):
    prompts = img_state.shape[1]
    img_rows = img_state.shape[2]
    txt_rows = txt_state.shape[2]
    width = img_state.shape[3]
    own = [jnp.concatenate([img_state[0, p], txt_state[0, p]], axis=0) for p in range(prompts)]
    pieces = []
    for rows in own:
        sent = after(rows, pieces[-1][2]) if pieces else rows
        pieces.append([rows, flip(rows, 1), flip(sent, 2)])
    for rows in pieces:
        rows.append(flip(rows[2], 1))
    shard = jnp.concatenate([w_up, w_down], axis=0)
    shards = [shard, flip(shard, 1, "req"), flip(shard, 2, "req")]
    shards.append(flip(after(shard, shards[2]), 3, "req"))
    shards += [flip(one, 1, "cfg") for one in shards]
    parts = modulation(cond_vec[0], w_mod)
    w_img = w_qkv_img.reshape(-1, width)
    w_txt = w_qkv_txt.reshape(-1, width)
    me = lax.axis_index("seq")
    starts = jnp.stack([txt_rows * (me ^ r) for r in range(4)]).astype(jnp.int32)
    near = project(
        [rows[r] for rows in pieces for r in (0, 1)],
        [p for p in range(prompts) for r in (0, 1)],
        img_rows, parts, w_img, w_txt,
    )
    outs = [w_attn_out, flip(w_attn_out, 1), flip(after(w_attn_out, pieces[-1][2]), 2)]
    outs.append(flip(outs[2], 1))
    attended = []
    for p in range(prompts):
        far = project(pieces[p][2:], [p, p], img_rows, parts, w_img, w_txt)
        attended.append(attention(p, text_len[0], starts, near, far, img_rows))
    results = []
    for p in range(prompts):
        heads = [attended[p], flip(attended[p], 1), flip(attended[p], 2)]
        heads.append(flip(heads[2], 1))
        heads[0] = after(heads[0], summed if results else attended[-1])
        keep, send, resid = tail(p, heads, outs, pieces[p], parts, shards, img_rows)
        core = flip(send, 1)
        summed = (
            keep[img_rows:].astype(jnp.float32) + core[img_rows:].astype(jnp.float32)
        ).astype(jnp.bfloat16)
        chip = flip(summed, 2)
        results += [resid, keep, core, chip]
    vmem = pl.BlockSpec(memory_space=pltpu.VMEM)
    branch_vel = pl.pallas_call(
        functools.partial(final_kernel, prompts, img_rows),
        out_shape=jax.ShapeDtypeStruct((prompts, img_rows, w_final.shape[1]), jnp.float32),
        in_specs=[vmem] * (4 * prompts + 2),
        out_specs=vmem,
        compiler_params=pltpu.CompilerParams(vmem_limit_bytes=VMEM_BYTES),
    )(*results, parts, w_final)
    return guide(branch_vel, latent)


def guide(branch_vel, latent):
    half_width = latent.shape[2]
    branch_index = lax.axis_index("cfg")
    own_half = lax.dynamic_slice_in_dim(branch_vel, branch_index * half_width, half_width, 2)
    other_half = lax.dynamic_slice_in_dim(
        branch_vel, (1 - branch_index) * half_width, half_width, 2
    )
    partner = partner_2(other_half.astype(jnp.bfloat16), "cfg", 0).astype(other_half.dtype)
    first = branch_index == 0
    cond_vel = jnp.where(first, own_half, partner)
    uncond_vel = jnp.where(first, partner, own_half)
    velocity = uncond_vel + 4.5 * (cond_vel - uncond_vel)
    latent_next = latent - 0.04 * velocity
    return (velocity, latent_next)


def plan(*shards):
    img_state, txt_state, w_qkv_img = shards[0], shards[1], shards[6]
    fits = (
        lax.axis_size("seq") == 4
        and lax.axis_size("req") == 4
        and lax.axis_size("cfg") == 2
        and shards[9].shape[0] % 16 == 0
        and img_state.shape[2] % 128 == 0
        and txt_state.shape[2] % 16 == 0
        and w_qkv_img.shape[1] % (2 * HEAD) == 0
    )
    return fast(*shards) if fits else local(*shards)


def solution(mesh):
    placed = (
        P("cfg", "req", "seq", None),
        P("cfg", "req", "seq", None),
        P("cfg", None, None),
        P("cfg", "req"),
        P("req", "seq", "cfg"),
        P(("req", "seq"), None),
        P(None, "seq", None),
        P(None, "seq", None),
        P("seq", None),
        P(("cfg", "req", "seq"), None),
        P(("cfg", "req", "seq"), None),
        P(),
    )
    return jax.shard_map(
        plan,
        mesh=mesh,
        in_specs=placed,
        out_specs=(P("req", "seq", "cfg"), P("req", "seq", "cfg")),
        check_vma=False,
    )
```

```python
import functools

import jax
import jax.numpy as jnp
from jax import lax
from jax.experimental import pallas as pl
from jax.experimental.pallas import tpu as pltpu
from jax.sharding import PartitionSpec as P

HEAD = 64
VMEM_BYTES = 56 * 1024 * 1024


def partner_2(shard, axis, apart):
    return lax.ppermute(shard, axis, [(i, i ^ 1 << apart) for i in range(lax.axis_size(axis))])


def layer_norm(value):
    mean = jnp.mean(value, axis=-1, keepdims=True)
    centered = value - mean
    spread = jnp.mean(centered * centered, axis=-1, keepdims=True)
    return centered * lax.rsqrt(spread + 1e-06)


def mlp_term(rows_in, up_block, down_block):
    inner = lax.dot_general(
        rows_in, up_block, (((1,), (1,)), ((), ())), preferred_element_type=jnp.float32
    )
    hidden = jax.nn.gelu(inner, approximate=True).astype(jnp.bfloat16)
    return jnp.dot(hidden, down_block, preferred_element_type=jnp.float32)


def local(
    img_state,
    txt_state,
    cond_vec,
    text_len,
    latent,
    w_mod,
    w_qkv_img,
    w_qkv_txt,
    w_attn_out,
    w_up,
    w_down,
    w_final,
):
    prompts_dev = img_state.shape[1]
    img_rows = img_state.shape[2]
    width = img_state.shape[3]
    cond_act = jax.nn.silu(cond_vec[0]).astype(jnp.bfloat16)
    mod_part = lax.dot_general(
        cond_act, w_mod, (((1,), (1,)), ((), ())), preferred_element_type=jnp.float32
    )
    mod_all = lax.all_gather(mod_part, ("req", "seq"), axis=1, tiled=True)
    mine = lax.dynamic_slice_in_dim(mod_all, lax.axis_index("req") * prompts_dev, prompts_dev, 0)
    parts = mine.reshape(prompts_dev, 10, 1, width)
    resid = img_state[0].astype(jnp.float32)
    a_img = (layer_norm(resid) * (1.0 + parts[:, 1]) + parts[:, 0]).astype(jnp.bfloat16)
    a_txt = (
        layer_norm(txt_state[0].astype(jnp.float32)) * (1.0 + parts[:, 7]) + parts[:, 6]
    ).astype(jnp.bfloat16)
    full_img, full_txt = (
        lax.all_gather(a_img, "seq", axis=1, tiled=True),
        lax.all_gather(a_txt, "seq", axis=1, tiled=True),
    )
    proj_img = jnp.einsum(
        "pnd,jed->jpne", full_img, w_qkv_img, preferred_element_type=jnp.float32
    ).astype(jnp.bfloat16)
    proj_txt = jnp.einsum(
        "pnd,jed->jpne", full_txt, w_qkv_txt, preferred_element_type=jnp.float32
    ).astype(jnp.bfloat16)
    total_img = full_img.shape[1]
    local_width = w_qkv_img.shape[1]
    heads_local = local_width // HEAD
    key_heads = jnp.concatenate([proj_img[1], proj_txt[1]], axis=1).reshape(
        prompts_dev, -1, heads_local, HEAD
    )
    value_heads = jnp.concatenate([proj_img[2], proj_txt[2]], axis=1).reshape(
        prompts_dev, -1, heads_local, HEAD
    )
    live = jnp.arange(key_heads.shape[1])[None, :] < (total_img + text_len[0])[:, None]
    block = min(512, total_img)
    queries = proj_img[0].reshape(prompts_dev, total_img // block, block, heads_local, HEAD)

    def attend(query):
        scores = jnp.einsum(
            "pqhe,pkhe->phqk", query, key_heads, preferred_element_type=jnp.float32
        ) * HEAD ** (-0.5)
        scores = jnp.where(live[:, None, None, :], scores, -1e30)
        probs = jax.nn.softmax(scores, axis=-1).astype(jnp.bfloat16)
        return jnp.einsum(
            "phqk,pkhe->pqhe", probs, value_heads, preferred_element_type=jnp.float32
        ).astype(jnp.bfloat16)

    attended = lax.map(attend, jnp.moveaxis(queries, 1, 0))
    attended = jnp.moveaxis(attended, 0, 1).reshape(prompts_dev, total_img, local_width)
    proj = jnp.swapaxes(
        lax.psum_scatter(
            jnp.einsum(
                "pnh,hd->npd", attended, w_attn_out, preferred_element_type=jnp.float32
            ).astype(jnp.bfloat16),
            "seq",
            scatter_dimension=0,
            tiled=True,
        ).astype(jnp.float32),
        0,
        1,
    )
    resid_one = (resid + parts[:, 2] * proj).astype(jnp.bfloat16)
    normed = (layer_norm(resid_one.astype(jnp.float32)) * (1.0 + parts[:, 4]) + parts[:, 3]).astype(
        jnp.bfloat16
    )
    own_rows = normed.reshape(prompts_dev * img_rows, width)
    both = lax.all_gather(own_rows, "cfg", axis=0, tiled=True)
    partial_out = mlp_term(
        both,
        lax.all_gather(w_up, ("req", "seq"), axis=0, tiled=True),
        lax.all_gather(w_down, ("req", "seq"), axis=0, tiled=True),
    )
    mlp_out = lax.psum_scatter(
        partial_out.astype(jnp.bfloat16), "cfg", scatter_dimension=0, tiled=True
    ).astype(jnp.float32)
    mlp_out = mlp_out.reshape(prompts_dev, img_rows, width)
    resid_two = resid_one.astype(jnp.float32) + parts[:, 5] * mlp_out
    final_in = (layer_norm(resid_two) * (1.0 + parts[:, 9]) + parts[:, 8]).astype(jnp.bfloat16)
    branch_vel = jnp.einsum("pnd,dc->pnc", final_in, w_final, preferred_element_type=jnp.float32)
    return guide(branch_vel, latent)

def flip(shard, bits, axis="seq"):
    return lax.ppermute(shard, axis, [(i, i ^ bits) for i in range(lax.axis_size(axis))])


def after(value, first):
    return lax.optimization_barrier((value, first))[0]


def norm_rows(rows, scale, shift):
    return (layer_norm(rows.astype(jnp.float32)) * (1.0 + scale) + shift).astype(jnp.bfloat16)


def across(left, right):
    return lax.dot_general(
        left, right, (((1,), (1,)), ((), ())), preferred_element_type=jnp.float32
    )


def mod_kernel(cond, weight, out, part, got, send_sem, recv_sem):
    reqs, seqs = lax.axis_size("req"), lax.axis_size("seq")
    group = reqs * seqs
    cfg, req = lax.axis_index("cfg"), lax.axis_index("req")
    me = req * seqs + lax.axis_index("seq")
    prompts = part.shape[1]
    barrier = pltpu.get_barrier_semaphore()
    for apart in range(1, group):
        peer = lax.rem(me + apart, group)
        pl.semaphore_signal(
            barrier,
            inc=1,
            device_id=(cfg, peer // seqs, lax.rem(peer, seqs)),
            device_id_type=pl.DeviceIdType.MESH,
        )
    rows = across(jax.nn.silu(cond[...]).astype(jnp.bfloat16), weight[...])
    for at in range(reqs):
        part[at] = rows[at * prompts : (at + 1) * prompts]
    pl.semaphore_wait(barrier, group - 1)
    copies = []
    for apart in range(1, group):
        peer = lax.rem(me + apart, group)
        copy = pltpu.make_async_remote_copy(
            src_ref=part.at[peer // seqs],
            dst_ref=got.at[me],
            send_sem=send_sem.at[apart],
            recv_sem=recv_sem.at[apart],
            device_id=(cfg, peer // seqs, lax.rem(peer, seqs)),
            device_id_type=pl.DeviceIdType.MESH,
        )
        copy.start()
        copies.append(copy)
    got[me] = part[req]
    for copy in copies:
        copy.wait()
    out[...] = got[...]


def modulation(cond, weight):
    reqs, seqs = lax.axis_size("req"), lax.axis_size("seq")
    group, prompts, columns = reqs * seqs, cond.shape[0] // reqs, weight.shape[0]
    vmem = pl.BlockSpec(memory_space=pltpu.VMEM)
    got = pl.pallas_call(
        mod_kernel,
        out_shape=jax.ShapeDtypeStruct((group, prompts, columns), jnp.float32),
        in_specs=[vmem, vmem],
        out_specs=vmem,
        scratch_shapes=[
            pltpu.VMEM((reqs, prompts, columns), jnp.float32),
            pltpu.VMEM((group, prompts, columns), jnp.float32),
            pltpu.SemaphoreType.DMA((group,)),
            pltpu.SemaphoreType.DMA((group,)),
        ],
        compiler_params=pltpu.CompilerParams(
            collective_id=0, has_side_effects=True, vmem_limit_bytes=VMEM_BYTES
        ),
        cost_estimate=pl.CostEstimate(
            flops=2 * cond.size * columns, bytes_accessed=2 * weight.size, transcendentals=0
        ),
    )(cond, weight)
    return jnp.swapaxes(got, 0, 1).reshape(prompts, 10, -1)


def qkv_kernel(owners, img_rows, txt_rows, *refs):
    count = len(owners)
    pieces = refs[:count]
    mod, w_img, w_txt, img_out, txt_out, txt_in = refs[count:]
    for at, (piece, owner) in enumerate(zip(pieces, owners)):
        img = norm_rows(piece[:img_rows], mod[owner, 1:2], mod[owner, 0:1])
        img_out[pl.ds(at * img_rows, img_rows)] = across(img, w_img[...]).astype(jnp.bfloat16)
        txt_in[pl.ds(at * txt_rows, txt_rows)] = norm_rows(
            piece[img_rows:], mod[owner, 7:8], mod[owner, 6:7]
        )
    txt_out[...] = across(txt_in[...], w_txt[...]).astype(jnp.bfloat16)


def project(pieces, owners, img_rows, parts, w_img, w_txt):
    count = len(pieces)
    txt_rows = pieces[0].shape[0] - img_rows
    width = pieces[0].shape[1]
    out = w_img.shape[0]
    rows = count * (img_rows + txt_rows)
    return pl.pallas_call(
        functools.partial(qkv_kernel, owners, img_rows, txt_rows),
        out_shape=(
            jax.ShapeDtypeStruct((count * img_rows, out), jnp.bfloat16),
            jax.ShapeDtypeStruct((count * txt_rows, out), jnp.bfloat16),
        ),
        in_specs=[pl.BlockSpec(memory_space=pltpu.VMEM)] * (count + 3),
        out_specs=(pl.BlockSpec(memory_space=pltpu.VMEM),) * 2,
        scratch_shapes=[pltpu.VMEM((count * txt_rows, width), jnp.bfloat16)],
        compiler_params=pltpu.CompilerParams(vmem_limit_bytes=VMEM_BYTES),
        cost_estimate=pl.CostEstimate(
            flops=2 * rows * width * out, bytes_accessed=4 * out * width, transcendentals=0
        ),
    )(*pieces, parts, w_img, w_txt)


def attend_kernel(
    txt_rows, prompt, length, starts, qa, qb, ka, kb, va, vb, tka, tkb, tva, tvb, out
):
    first = lax.broadcasted_iota(jnp.int32, (1, 2 * HEAD), 1) < HEAD
    column = lax.broadcasted_iota(jnp.int32, (1, 2 * txt_rows), 1)
    live = []
    for base in (0, 2):
        slot = jnp.where(
            column < txt_rows, starts[base] + column, starts[base + 1] + column - txt_rows
        )
        live.append(slot < length[prompt])
    keys = (ka[...], kb[...], tka[...], tkb[...])
    values = (va[...], vb[...], tva[...], tvb[...])
    one = jnp.ones((), jnp.bfloat16)
    zero = jnp.zeros((), jnp.bfloat16)
    held = [
        [jnp.where(first, value, one) for value in values],
        [jnp.where(first, one, value) for value in values],
    ]
    for side, q_ref in enumerate((qa, qb)):
        query = q_ref[...] * jnp.asarray(HEAD ** (-0.5), jnp.bfloat16)
        sums = []
        for head in range(2):
            masked = jnp.where(first, query, zero) if head == 0 else jnp.where(first, zero, query)
            scores = [across(masked, key) for key in keys]
            for text in range(2):
                scores[2 + text] = jnp.where(live[text], scores[2 + text], -1e30)
            top = functools.reduce(
                jnp.maximum, [jnp.max(score, axis=-1, keepdims=True) for score in scores]
            )
            total = None
            for score, value in zip(scores, held[head]):
                weight = jnp.exp(score - top).astype(jnp.bfloat16)
                term = jnp.dot(weight, value, preferred_element_type=jnp.float32)
                total = term if total is None else total + term
            sums.append(total)
        out[0, side] = jnp.where(
            first, sums[0] / sums[0][:, HEAD : HEAD + 1], sums[1] / sums[1][:, 0:1]
        ).astype(jnp.bfloat16)


def attention(prompt, length, starts, near, far, img_rows):
    img_near, txt_near = near
    img_far, txt_far = far
    lanes = 2 * HEAD
    pairs = img_near.shape[1] // (3 * lanes)
    txt_rows = txt_far.shape[0] // 2
    half = 2 * img_rows
    smem = pl.BlockSpec(memory_space=pltpu.SMEM)

    def spec(rows, row_of, third):
        return pl.BlockSpec((rows, lanes), lambda j, i: (row_of(i), third * pairs + j))

    specs = [smem, smem]
    specs += [spec(img_rows, lambda i: 2 * prompt + i, 0), spec(img_rows, lambda i: i, 0)]
    for third in (1, 2):
        specs += [spec(half, lambda i: prompt, third), spec(half, lambda i: 0, third)]
    for third in (1, 2):
        specs += [
            spec(2 * txt_rows, lambda i: prompt, third),
            spec(2 * txt_rows, lambda i: 0, third),
        ]
    keys = 2 * half + 4 * txt_rows
    out = pl.pallas_call(
        functools.partial(attend_kernel, txt_rows, prompt),
        grid=(pairs, 2),
        out_shape=jax.ShapeDtypeStruct((2, 2, img_rows, pairs * lanes), jnp.bfloat16),
        in_specs=specs,
        out_specs=pl.BlockSpec((1, 2, img_rows, lanes), lambda j, i: (i, 0, 0, j)),
        compiler_params=pltpu.CompilerParams(vmem_limit_bytes=VMEM_BYTES),
        cost_estimate=pl.CostEstimate(
            flops=16 * 2 * half * keys * pairs * lanes,
            bytes_accessed=8 * half * pairs * lanes,
            transcendentals=2 * half * keys * pairs * 2,
        ),
    )(
        length, starts,
        img_near, img_far, img_near, img_far, img_near, img_far,
        txt_near, txt_far, txt_near, txt_far,
    )
    return out.reshape(2 * half, pairs * lanes)


def tail_kernel(*refs):
    (own_next, first_heads, outs, pieces, up_in, downs), refs = take(refs, 1, 4, 4, 8, 1, 8)
    mod, w_final, out = refs[:3]
    heads, states, wo, up, down, send, core, base, chip_send, chip, resids = refs[3:14]
    local_sem, send_sem, recv_sem = refs[14:]
    step = pl.program_id(0)
    prompt, half = step // 2, 1 - lax.rem(step, 2)
    img_rows = states.shape[2]
    two = 2 * img_rows
    cfg, req, me = (lax.axis_index(name) for name in ("cfg", "req", "seq"))
    reqs = lax.axis_size("req")
    near, far = me ^ 1, me ^ 2
    units = downs[0].shape[0]

    def remote(at, source, target, seq):
        return pltpu.make_async_remote_copy(
            src_ref=source,
            dst_ref=target,
            send_sem=send_sem.at[at],
            recv_sem=recv_sem.at[at],
            device_id=(cfg, req, seq),
            device_id_type=pl.DeviceIdType.MESH,
        )

    heads_near = remote(0, own_next[0], heads.at[1, 1], near)
    heads_far = remote(1, own_next[0], heads.at[1, 2], far)
    heads_relay = remote(2, heads.at[1, 2], heads.at[1, 3], near)
    to_core = [remote(3 + p, send.at[p], core.at[p], near) for p in range(2)]
    to_chip = [remote(5 + p, chip_send.at[p], chip.at[p], far) for p in range(2)]

    pairs = [(first_heads[r], heads.at[0, r]) for r in range(4)]
    pairs += [(pieces[4 * p + r].at[pl.ds(0, img_rows)], states.at[p, r]) for p in (0, 1) for r in range(4)]
    pairs += [(outs[r], wo.at[r]) for r in range(4)]
    early = len(pairs)
    pairs += [(own_next[0], heads.at[1, 0]), (up_in[0], up)]
    for at, shard in enumerate(downs):
        place = ((cfg ^ (at // 4)) * reqs + (req ^ (at % 4))) * units
        pairs.append((shard, down.at[pl.ds(pl.multiple_of(place, units), units)]))
    loads = [
        pltpu.make_async_copy(source, target, local_sem.at[at])
        for at, (source, target) in enumerate(pairs)
    ]

    @pl.when(step == 0)
    def _():
        barrier = pltpu.get_barrier_semaphore()
        for seq in (near, far):
            pl.semaphore_signal(
                barrier, inc=1, device_id=(cfg, req, seq), device_id_type=pl.DeviceIdType.MESH
            )
        for load in loads:
            load.start()
        pl.semaphore_wait(barrier, 2)
        heads_far.start()
        heads_near.start()
        for load in loads[:early]:
            load.wait()

    @pl.when(step == 2)
    def _():
        heads_near.wait()
        heads_relay.wait()

    proj = None
    for r in range(4):
        rows = heads[prompt, r, half ^ (r % 2)]
        if r >= 2:
            rows = jnp.concatenate([rows[img_rows:], rows[:img_rows]], axis=0)
        term = jnp.dot(rows, wo[r], preferred_element_type=jnp.float32)
        proj = term if proj is None else proj + term
    state = jnp.concatenate([states[prompt, half], states[prompt, half + 2]], axis=0)
    resid = (state.astype(jnp.float32) + mod[prompt, 2:3] * proj).astype(jnp.bfloat16)
    normed = norm_rows(resid, mod[prompt, 4:5], mod[prompt, 3:4])

    @pl.when(step == 0)
    def _():
        for load in loads[early:]:
            load.wait()

    cut = 512
    total = None
    for start in range(0, up.shape[0], cut):
        inner = across(normed, up[pl.ds(start, cut)])
        hidden = jax.nn.gelu(inner, approximate=True).astype(jnp.bfloat16)
        term = jnp.dot(hidden, down[pl.ds(start, cut)], preferred_element_type=jnp.float32)
        total = term if total is None else total + term

    for p in range(2):

        @pl.when(step == 2 * p)
        def _():
            send[p] = total.astype(jnp.bfloat16)
            to_core[p].start()

        @pl.when(step == 2 * p + 1)
        def _():
            to_core[p].wait()
            chip_send[p] = (total[img_rows:] + core[p, img_rows:].astype(jnp.float32)).astype(
                jnp.bfloat16
            )
            to_chip[p].start()
            base[p] = total[:img_rows] + core[p, :img_rows].astype(jnp.float32)
            resids[p] = resid[:img_rows]

    @pl.when(step == 0)
    def _():
        heads_far.wait()
        heads_relay.start()

    @pl.when(step == 3)
    def _():
        for p in range(2):
            to_chip[p].wait()
            mlp = base[p] + chip[p].astype(jnp.float32)
            two_sum = resids[p].astype(jnp.float32) + mod[p, 5:6] * mlp
            last = norm_rows(two_sum, mod[p, 9:10], mod[p, 8:9])
            out[p] = jnp.dot(last, w_final[...], preferred_element_type=jnp.float32)


def take(refs, *counts):
    groups = []
    for count in counts:
        groups.append(refs[:count])
        refs = refs[count:]
    return groups, refs


def tail(own_next, first_heads, outs, pieces, up, downs, parts, w_final, img_rows):
    width = parts.shape[2]
    local_width = outs[0].shape[0]
    units = up.shape[0]
    two = 2 * img_rows
    split = [rows.reshape(2, two, local_width) for rows in [own_next] + first_heads]
    vmem = pl.BlockSpec(memory_space=pltpu.VMEM)
    anywhere = pl.BlockSpec(memory_space=pl.ANY)
    bf16, f32 = jnp.bfloat16, jnp.float32
    rows = 8 * img_rows
    operands = split + outs + pieces + [up] + downs
    loads = len(operands)
    return pl.pallas_call(
        tail_kernel,
        grid=(4,),
        out_shape=jax.ShapeDtypeStruct((2, img_rows, w_final.shape[1]), f32),
        in_specs=[anywhere] * loads + [vmem, vmem],
        out_specs=vmem,
        scratch_shapes=[
            pltpu.VMEM((2, 4, 2, two, local_width), bf16),
            pltpu.VMEM((2, 4, img_rows, width), bf16),
            pltpu.VMEM((4, local_width, width), bf16),
            pltpu.VMEM((units, width), bf16),
            pltpu.VMEM((units, width), bf16),
            pltpu.VMEM((2, two, width), bf16),
            pltpu.VMEM((2, two, width), bf16),
            pltpu.VMEM((2, img_rows, width), f32),
            pltpu.VMEM((2, img_rows, width), bf16),
            pltpu.VMEM((2, img_rows, width), bf16),
            pltpu.VMEM((2, img_rows, width), bf16),
            pltpu.SemaphoreType.DMA((loads,)),
            pltpu.SemaphoreType.DMA((7,)),
            pltpu.SemaphoreType.DMA((7,)),
        ],
        compiler_params=pltpu.CompilerParams(
            collective_id=1, has_side_effects=True, vmem_limit_bytes=VMEM_BYTES
        ),
        cost_estimate=pl.CostEstimate(
            flops=2 * rows * width * (width + 2 * units),
            bytes_accessed=2 * width * (width + 2 * units) + 8 * rows * width,
            transcendentals=rows * units,
        ),
    )(*operands, parts, w_final)


def fast(
    img_state,
    txt_state,
    cond_vec,
    text_len,
    latent,
    w_mod,
    w_qkv_img,
    w_qkv_txt,
    w_attn_out,
    w_up,
    w_down,
    w_final,
):
    prompts = img_state.shape[1]
    img_rows = img_state.shape[2]
    txt_rows = txt_state.shape[2]
    width = img_state.shape[3]
    parts = modulation(cond_vec[0], w_mod)
    own = [
        after(jnp.concatenate([img_state[0, p], txt_state[0, p]], axis=0), parts)
        for p in range(prompts)
    ]
    pieces = []
    for rows in own:
        sent = after(rows, pieces[-1][2]) if pieces else rows
        pieces.append([rows, flip(rows, 1), flip(sent, 2)])
    for rows in pieces:
        rows.append(flip(rows[2], 1))
    up = lax.all_gather(after(w_up, parts), ("cfg", "req"), axis=0, tiled=True)
    first = after(w_down, parts)
    downs = [first] + [flip(first, bits, "req") for bits in (1, 2, 3)]
    downs += [flip(one, 1, "cfg") for one in downs]
    w_img = w_qkv_img.reshape(-1, width)
    w_txt = w_qkv_txt.reshape(-1, width)
    me = lax.axis_index("seq")
    starts = jnp.stack([txt_rows * (me ^ r) for r in range(4)]).astype(jnp.int32)
    near = project(
        [rows[r] for rows in pieces for r in (0, 1)],
        [p for p in range(prompts) for r in (0, 1)],
        img_rows, parts, w_img, w_txt,
    )
    outs = [w_attn_out, flip(w_attn_out, 1), flip(after(w_attn_out, pieces[-1][2]), 2)]
    outs.append(flip(outs[2], 1))
    attended = []
    for p in range(prompts):
        far = project(pieces[p][2:], [p, p], img_rows, parts, w_img, w_txt)
        attended.append(attention(p, text_len[0], starts, near, far, img_rows))
    heads = [attended[0], flip(attended[0], 1), flip(attended[0], 2)]
    heads.append(flip(heads[2], 1))
    branch_vel = tail(
        attended[1], heads, outs, pieces[0] + pieces[1], up, downs, parts, w_final, img_rows
    )
    return guide(branch_vel, latent)


def guide(branch_vel, latent):
    half_width = latent.shape[2]
    branch_index = lax.axis_index("cfg")
    own_half = lax.dynamic_slice_in_dim(branch_vel, branch_index * half_width, half_width, 2)
    other_half = lax.dynamic_slice_in_dim(
        branch_vel, (1 - branch_index) * half_width, half_width, 2
    )
    partner = partner_2(other_half.astype(jnp.bfloat16), "cfg", 0).astype(other_half.dtype)
    first = branch_index == 0
    cond_vel = jnp.where(first, own_half, partner)
    uncond_vel = jnp.where(first, partner, own_half)
    velocity = uncond_vel + 4.5 * (cond_vel - uncond_vel)
    latent_next = latent - 0.04 * velocity
    return (velocity, latent_next)


def plan(*shards):
    img_state, txt_state, w_qkv_img = shards[0], shards[1], shards[6]
    fits = (
        lax.axis_size("seq") == 4
        and lax.axis_size("req") == 4
        and lax.axis_size("cfg") == 2
        and img_state.shape[1] == 2
        and shards[9].shape[0] % 16 == 0
        and img_state.shape[2] % 128 == 0
        and txt_state.shape[2] % 16 == 0
        and w_qkv_img.shape[1] % (2 * HEAD) == 0
    )
    return fast(*shards) if fits else local(*shards)


def solution(mesh):
    placed = (
        P("cfg", "req", "seq", None),
        P("cfg", "req", "seq", None),
        P("cfg", None, None),
        P("cfg", "req"),
        P("req", "seq", "cfg"),
        P(("req", "seq"), None),
        P(None, "seq", None),
        P(None, "seq", None),
        P("seq", None),
        P(("cfg", "req", "seq"), None),
        P(("cfg", "req", "seq"), None),
        P(),
    )
    return jax.shard_map(
        plan,
        mesh=mesh,
        in_specs=placed,
        out_specs=(P("req", "seq", "cfg"), P("req", "seq", "cfg")),
        check_vma=False,
    )
```

```python
import functools

import jax
import jax.numpy as jnp
from jax import lax
from jax.experimental import pallas as pl
from jax.experimental.pallas import tpu as pltpu
from jax.sharding import PartitionSpec as P

HEAD = 64
VMEM_BYTES = 56 * 1024 * 1024


def partner_2(shard, axis, apart):
    return lax.ppermute(shard, axis, [(i, i ^ 1 << apart) for i in range(lax.axis_size(axis))])


def layer_norm(value):
    mean = jnp.mean(value, axis=-1, keepdims=True)
    centered = value - mean
    spread = jnp.mean(centered * centered, axis=-1, keepdims=True)
    return centered * lax.rsqrt(spread + 1e-06)


def mlp_term(rows_in, up_block, down_block):
    inner = lax.dot_general(
        rows_in, up_block, (((1,), (1,)), ((), ())), preferred_element_type=jnp.float32
    )
    hidden = jax.nn.gelu(inner, approximate=True).astype(jnp.bfloat16)
    return jnp.dot(hidden, down_block, preferred_element_type=jnp.float32)


def local(
    img_state,
    txt_state,
    cond_vec,
    text_len,
    latent,
    w_mod,
    w_qkv_img,
    w_qkv_txt,
    w_attn_out,
    w_up,
    w_down,
    w_final,
):
    prompts_dev = img_state.shape[1]
    img_rows = img_state.shape[2]
    width = img_state.shape[3]
    cond_act = jax.nn.silu(cond_vec[0]).astype(jnp.bfloat16)
    mod_part = lax.dot_general(
        cond_act, w_mod, (((1,), (1,)), ((), ())), preferred_element_type=jnp.float32
    )
    mod_all = lax.all_gather(mod_part, ("req", "seq"), axis=1, tiled=True)
    mine = lax.dynamic_slice_in_dim(mod_all, lax.axis_index("req") * prompts_dev, prompts_dev, 0)
    parts = mine.reshape(prompts_dev, 10, 1, width)
    resid = img_state[0].astype(jnp.float32)
    a_img = (layer_norm(resid) * (1.0 + parts[:, 1]) + parts[:, 0]).astype(jnp.bfloat16)
    a_txt = (
        layer_norm(txt_state[0].astype(jnp.float32)) * (1.0 + parts[:, 7]) + parts[:, 6]
    ).astype(jnp.bfloat16)
    full_img, full_txt = (
        lax.all_gather(a_img, "seq", axis=1, tiled=True),
        lax.all_gather(a_txt, "seq", axis=1, tiled=True),
    )
    proj_img = jnp.einsum(
        "pnd,jed->jpne", full_img, w_qkv_img, preferred_element_type=jnp.float32
    ).astype(jnp.bfloat16)
    proj_txt = jnp.einsum(
        "pnd,jed->jpne", full_txt, w_qkv_txt, preferred_element_type=jnp.float32
    ).astype(jnp.bfloat16)
    total_img = full_img.shape[1]
    local_width = w_qkv_img.shape[1]
    heads_local = local_width // HEAD
    key_heads = jnp.concatenate([proj_img[1], proj_txt[1]], axis=1).reshape(
        prompts_dev, -1, heads_local, HEAD
    )
    value_heads = jnp.concatenate([proj_img[2], proj_txt[2]], axis=1).reshape(
        prompts_dev, -1, heads_local, HEAD
    )
    live = jnp.arange(key_heads.shape[1])[None, :] < (total_img + text_len[0])[:, None]
    block = min(512, total_img)
    queries = proj_img[0].reshape(prompts_dev, total_img // block, block, heads_local, HEAD)

    def attend(query):
        scores = jnp.einsum(
            "pqhe,pkhe->phqk", query, key_heads, preferred_element_type=jnp.float32
        ) * HEAD ** (-0.5)
        scores = jnp.where(live[:, None, None, :], scores, -1e30)
        probs = jax.nn.softmax(scores, axis=-1).astype(jnp.bfloat16)
        return jnp.einsum(
            "phqk,pkhe->pqhe", probs, value_heads, preferred_element_type=jnp.float32
        ).astype(jnp.bfloat16)

    attended = lax.map(attend, jnp.moveaxis(queries, 1, 0))
    attended = jnp.moveaxis(attended, 0, 1).reshape(prompts_dev, total_img, local_width)
    proj = jnp.swapaxes(
        lax.psum_scatter(
            jnp.einsum(
                "pnh,hd->npd", attended, w_attn_out, preferred_element_type=jnp.float32
            ).astype(jnp.bfloat16),
            "seq",
            scatter_dimension=0,
            tiled=True,
        ).astype(jnp.float32),
        0,
        1,
    )
    resid_one = (resid + parts[:, 2] * proj).astype(jnp.bfloat16)
    normed = (layer_norm(resid_one.astype(jnp.float32)) * (1.0 + parts[:, 4]) + parts[:, 3]).astype(
        jnp.bfloat16
    )
    own_rows = normed.reshape(prompts_dev * img_rows, width)
    both = lax.all_gather(own_rows, "cfg", axis=0, tiled=True)
    partial_out = mlp_term(
        both,
        lax.all_gather(w_up, ("req", "seq"), axis=0, tiled=True),
        lax.all_gather(w_down, ("req", "seq"), axis=0, tiled=True),
    )
    mlp_out = lax.psum_scatter(
        partial_out.astype(jnp.bfloat16), "cfg", scatter_dimension=0, tiled=True
    ).astype(jnp.float32)
    mlp_out = mlp_out.reshape(prompts_dev, img_rows, width)
    resid_two = resid_one.astype(jnp.float32) + parts[:, 5] * mlp_out
    final_in = (layer_norm(resid_two) * (1.0 + parts[:, 9]) + parts[:, 8]).astype(jnp.bfloat16)
    branch_vel = jnp.einsum("pnd,dc->pnc", final_in, w_final, preferred_element_type=jnp.float32)
    return guide(branch_vel, latent)

def flip(shard, bits, axis="seq"):
    return lax.ppermute(shard, axis, [(i, i ^ bits) for i in range(lax.axis_size(axis))])


def after(value, first):
    return lax.optimization_barrier((value, first))[0]


def norm_rows(rows, scale, shift):
    return (layer_norm(rows.astype(jnp.float32)) * (1.0 + scale) + shift).astype(jnp.bfloat16)


def across(left, right):
    return lax.dot_general(
        left, right, (((1,), (1,)), ((), ())), preferred_element_type=jnp.float32
    )


def mod_kernel(cond, weight, out, part, got, send_sem, recv_sem):
    reqs, seqs = lax.axis_size("req"), lax.axis_size("seq")
    group = reqs * seqs
    cfg, req = lax.axis_index("cfg"), lax.axis_index("req")
    me = req * seqs + lax.axis_index("seq")
    prompts = part.shape[1]
    barrier = pltpu.get_barrier_semaphore()
    for apart in range(1, group):
        peer = lax.rem(me + apart, group)
        pl.semaphore_signal(
            barrier,
            inc=1,
            device_id=(cfg, peer // seqs, lax.rem(peer, seqs)),
            device_id_type=pl.DeviceIdType.MESH,
        )
    rows = across(jax.nn.silu(cond[...]).astype(jnp.bfloat16), weight[...])
    for at in range(reqs):
        part[at] = rows[at * prompts : (at + 1) * prompts]
    pl.semaphore_wait(barrier, group - 1)
    copies = []
    for apart in range(1, group):
        peer = lax.rem(me + apart, group)
        copy = pltpu.make_async_remote_copy(
            src_ref=part.at[peer // seqs],
            dst_ref=got.at[me],
            send_sem=send_sem.at[apart],
            recv_sem=recv_sem.at[apart],
            device_id=(cfg, peer // seqs, lax.rem(peer, seqs)),
            device_id_type=pl.DeviceIdType.MESH,
        )
        copy.start()
        copies.append(copy)
    got[me] = part[req]
    for copy in copies:
        copy.wait()
    out[...] = got[...]


def modulation(cond, weight):
    reqs, seqs = lax.axis_size("req"), lax.axis_size("seq")
    group, prompts, columns = reqs * seqs, cond.shape[0] // reqs, weight.shape[0]
    vmem = pl.BlockSpec(memory_space=pltpu.VMEM)
    got = pl.pallas_call(
        mod_kernel,
        out_shape=jax.ShapeDtypeStruct((group, prompts, columns), jnp.float32),
        in_specs=[vmem, vmem],
        out_specs=vmem,
        scratch_shapes=[
            pltpu.VMEM((reqs, prompts, columns), jnp.float32),
            pltpu.VMEM((group, prompts, columns), jnp.float32),
            pltpu.SemaphoreType.DMA((group,)),
            pltpu.SemaphoreType.DMA((group,)),
        ],
        compiler_params=pltpu.CompilerParams(
            collective_id=0, has_side_effects=True, vmem_limit_bytes=VMEM_BYTES
        ),
    )(cond, weight)
    return jnp.swapaxes(got, 0, 1).reshape(prompts, 10, -1)


def qkv_kernel(owners, img_rows, txt_rows, *refs):
    count = len(owners)
    pieces = refs[:count]
    mod, w_img, w_txt, img_out, txt_out, txt_in = refs[count:]
    for at, (piece, owner) in enumerate(zip(pieces, owners)):
        img = norm_rows(piece[:img_rows], mod[owner, 1:2], mod[owner, 0:1])
        img_out[pl.ds(at * img_rows, img_rows)] = across(img, w_img[...]).astype(jnp.bfloat16)
        txt_in[pl.ds(at * txt_rows, txt_rows)] = norm_rows(
            piece[img_rows:], mod[owner, 7:8], mod[owner, 6:7]
        )
    txt_out[...] = across(txt_in[...], w_txt[...]).astype(jnp.bfloat16)


def project(pieces, owners, img_rows, parts, w_img, w_txt):
    count = len(pieces)
    txt_rows = pieces[0].shape[0] - img_rows
    width = pieces[0].shape[1]
    out = w_img.shape[0]
    rows = count * (img_rows + txt_rows)
    return pl.pallas_call(
        functools.partial(qkv_kernel, owners, img_rows, txt_rows),
        out_shape=(
            jax.ShapeDtypeStruct((count * img_rows, out), jnp.bfloat16),
            jax.ShapeDtypeStruct((count * txt_rows, out), jnp.bfloat16),
        ),
        in_specs=[pl.BlockSpec(memory_space=pltpu.VMEM)] * (count + 3),
        out_specs=(pl.BlockSpec(memory_space=pltpu.VMEM),) * 2,
        scratch_shapes=[pltpu.VMEM((count * txt_rows, width), jnp.bfloat16)],
        compiler_params=pltpu.CompilerParams(vmem_limit_bytes=VMEM_BYTES),
    )(*pieces, parts, w_img, w_txt)


def attend_kernel(
    txt_rows, prompt, length, starts, qa, qb, ka, kb, va, vb, tka, tkb, tva, tvb, out
):
    first = lax.broadcasted_iota(jnp.int32, (1, 2 * HEAD), 1) < HEAD
    column = lax.broadcasted_iota(jnp.int32, (1, 2 * txt_rows), 1)
    live = []
    for base in (0, 2):
        slot = jnp.where(
            column < txt_rows, starts[base] + column, starts[base + 1] + column - txt_rows
        )
        live.append(slot < length[prompt])
    keys = (ka[...], kb[...], tka[...], tkb[...])
    values = (va[...], vb[...], tva[...], tvb[...])
    one = jnp.ones((), jnp.bfloat16)
    zero = jnp.zeros((), jnp.bfloat16)
    held = [
        [jnp.where(first, value, one) for value in values],
        [jnp.where(first, one, value) for value in values],
    ]
    for side, q_ref in enumerate((qa, qb)):
        query = q_ref[...] * jnp.asarray(HEAD ** (-0.5), jnp.bfloat16)
        sums = []
        for head in range(2):
            masked = jnp.where(first, query, zero) if head == 0 else jnp.where(first, zero, query)
            scores = [across(masked, key) for key in keys]
            for text in range(2):
                scores[2 + text] = jnp.where(live[text], scores[2 + text], -1e30)
            top = functools.reduce(
                jnp.maximum, [jnp.max(score, axis=-1, keepdims=True) for score in scores]
            )
            total = None
            for score, value in zip(scores, held[head]):
                weight = jnp.exp(score - top).astype(jnp.bfloat16)
                term = jnp.dot(weight, value, preferred_element_type=jnp.float32)
                total = term if total is None else total + term
            sums.append(total)
        out[0, side] = jnp.where(
            first, sums[0] / sums[0][:, HEAD : HEAD + 1], sums[1] / sums[1][:, 0:1]
        ).astype(jnp.bfloat16)


def attention(prompt, length, starts, near, far, img_rows):
    img_near, txt_near = near
    img_far, txt_far = far
    lanes = 2 * HEAD
    pairs = img_near.shape[1] // (3 * lanes)
    txt_rows = txt_far.shape[0] // 2
    half = 2 * img_rows
    smem = pl.BlockSpec(memory_space=pltpu.SMEM)

    def spec(rows, row_of, third):
        return pl.BlockSpec((rows, lanes), lambda j, i: (row_of(i), third * pairs + j))

    specs = [smem, smem]
    specs += [spec(img_rows, lambda i: 2 * prompt + i, 0), spec(img_rows, lambda i: i, 0)]
    for third in (1, 2):
        specs += [spec(half, lambda i: prompt, third), spec(half, lambda i: 0, third)]
    for third in (1, 2):
        specs += [
            spec(2 * txt_rows, lambda i: prompt, third),
            spec(2 * txt_rows, lambda i: 0, third),
        ]
    keys = 2 * half + 4 * txt_rows
    out = pl.pallas_call(
        functools.partial(attend_kernel, txt_rows, prompt),
        grid=(pairs, 2),
        out_shape=jax.ShapeDtypeStruct((2, 2, img_rows, pairs * lanes), jnp.bfloat16),
        in_specs=specs,
        out_specs=pl.BlockSpec((1, 2, img_rows, lanes), lambda j, i: (i, 0, 0, j)),
        compiler_params=pltpu.CompilerParams(vmem_limit_bytes=VMEM_BYTES),
    )(
        length, starts,
        img_near, img_far, img_near, img_far, img_near, img_far,
        txt_near, txt_far, txt_near, txt_far,
    )
    return out.reshape(2 * half, pairs * lanes)


def attn_out_kernel(prompt, img_rows, *refs):
    (heads, outs, pieces), refs = take(refs, 4, 4, 4)
    mod, normed, resid_out, state = refs
    step = pl.program_id(0)
    for half in range(2):

        @pl.when(step == 1 - half)
        def _():
            state[:img_rows] = pieces[half][:img_rows]
            state[img_rows:] = pieces[half + 2][:img_rows]

    proj = None
    for r in range(4):
        rows = heads[r][...]
        if r >= 2:
            rows = jnp.concatenate([rows[img_rows:], rows[:img_rows]], axis=0)
        term = jnp.dot(rows, outs[r][...], preferred_element_type=jnp.float32)
        proj = term if proj is None else proj + term
    resid = (state[...].astype(jnp.float32) + mod[prompt, 2:3] * proj).astype(jnp.bfloat16)
    normed[...] = norm_rows(resid, mod[prompt, 4:5], mod[prompt, 3:4])
    resid_out[...] = resid[:img_rows]


def attn_out(prompt, heads, outs, pieces, parts, img_rows):
    width = parts.shape[2]
    local_width = heads[0].shape[1]
    two = 2 * img_rows

    def spec(apart):
        return pl.BlockSpec((two, local_width), lambda t: ((1 - t) ^ (apart % 2), 0))

    vmem = pl.BlockSpec(memory_space=pltpu.VMEM)
    return pl.pallas_call(
        functools.partial(attn_out_kernel, prompt, img_rows),
        grid=(2,),
        out_shape=(
            jax.ShapeDtypeStruct((2 * two, width), jnp.bfloat16),
            jax.ShapeDtypeStruct((img_rows, width), jnp.bfloat16),
        ),
        in_specs=[spec(r) for r in range(4)] + [vmem] * 9,
        out_specs=(
            pl.BlockSpec((two, width), lambda t: (1 - t, 0)),
            pl.BlockSpec((img_rows, width), lambda t: (0, 0)),
        ),
        scratch_shapes=[pltpu.VMEM((two, width), jnp.bfloat16)],
        compiler_params=pltpu.CompilerParams(vmem_limit_bytes=40 * 1024 * 1024),
    )(*heads, *outs, *pieces, parts)


def tail_kernel(*refs):
    (normed_in, resid_in, up_in, downs), refs = take(refs, 2, 2, 1, 8)
    mod, w_final, out = refs[:3]
    normeds, resids, up, down, send, core, base, chip_send, chip = refs[3:12]
    local_sem, send_sem, recv_sem = refs[12:]
    step = pl.program_id(0)
    prompt, half = step // 2, 1 - lax.rem(step, 2)
    img_rows = resids.shape[1]
    cfg, req, me = (lax.axis_index(name) for name in ("cfg", "req", "seq"))
    reqs = lax.axis_size("req")
    near, far = me ^ 1, me ^ 2
    units = downs[0].shape[0]

    def remote(at, source, target, seq):
        return pltpu.make_async_remote_copy(
            src_ref=source,
            dst_ref=target,
            send_sem=send_sem.at[at],
            recv_sem=recv_sem.at[at],
            device_id=(cfg, req, seq),
            device_id_type=pl.DeviceIdType.MESH,
        )

    to_core = [remote(p, send.at[p], core.at[p], near) for p in range(2)]
    to_chip = [remote(2 + p, chip_send.at[p], chip.at[p], far) for p in range(2)]

    pairs = [(normed_in[0], normeds.at[0]), (up_in[0], up)]
    for at, shard in enumerate(downs):
        place = ((cfg ^ (at // 4)) * reqs + (req ^ (at % 4))) * units
        pairs.append((shard, down.at[pl.ds(pl.multiple_of(place, units), units)]))
    early = len(pairs)
    pairs += [(normed_in[1], normeds.at[1])]
    pairs += [(resid_in[p], resids.at[p]) for p in range(2)]
    loads = [
        pltpu.make_async_copy(source, target, local_sem.at[at])
        for at, (source, target) in enumerate(pairs)
    ]

    @pl.when(step == 0)
    def _():
        barrier = pltpu.get_barrier_semaphore()
        for seq in (near, far):
            pl.semaphore_signal(
                barrier, inc=1, device_id=(cfg, req, seq), device_id_type=pl.DeviceIdType.MESH
            )
        for load in loads:
            load.start()
        pl.semaphore_wait(barrier, 2)
        for load in loads[:early]:
            load.wait()

    @pl.when(step == 1)
    def _():
        for load in loads[early:]:
            load.wait()

    normed = normeds[prompt, half]
    cut = 512
    total = None
    for start in range(0, up.shape[0], cut):
        inner = across(normed, up[pl.ds(start, cut)])
        hidden = jax.nn.gelu(inner, approximate=True).astype(jnp.bfloat16)
        term = jnp.dot(hidden, down[pl.ds(start, cut)], preferred_element_type=jnp.float32)
        total = term if total is None else total + term

    for p in range(2):

        @pl.when(step == 2 * p)
        def _():
            send[p] = total.astype(jnp.bfloat16)
            to_core[p].start()

        @pl.when(step == 2 * p + 1)
        def _():
            to_core[p].wait()
            chip_send[p] = (total[img_rows:] + core[p, img_rows:].astype(jnp.float32)).astype(
                jnp.bfloat16
            )
            to_chip[p].start()
            base[p] = total[:img_rows] + core[p, :img_rows].astype(jnp.float32)

    @pl.when(step == 3)
    def _():
        for p in range(2):
            to_chip[p].wait()
            mlp = base[p] + chip[p].astype(jnp.float32)
            two_sum = resids[p].astype(jnp.float32) + mod[p, 5:6] * mlp
            last = norm_rows(two_sum, mod[p, 9:10], mod[p, 8:9])
            out[p] = jnp.dot(last, w_final[...], preferred_element_type=jnp.float32)


def take(refs, *counts):
    groups = []
    for count in counts:
        groups.append(refs[:count])
        refs = refs[count:]
    return groups, refs


def tail(normed, resids, up, downs, parts, w_final):
    width = parts.shape[2]
    img_rows = resids[0].shape[0]
    units = up.shape[0]
    two = 2 * img_rows
    split = [rows.reshape(2, two, width) for rows in normed]
    vmem = pl.BlockSpec(memory_space=pltpu.VMEM)
    anywhere = pl.BlockSpec(memory_space=pl.ANY)
    bf16, f32 = jnp.bfloat16, jnp.float32
    rows = 8 * img_rows
    operands = split + resids + [up] + downs
    loads = len(operands)
    return pl.pallas_call(
        tail_kernel,
        grid=(4,),
        out_shape=jax.ShapeDtypeStruct((2, img_rows, w_final.shape[1]), f32),
        in_specs=[anywhere] * loads + [vmem, vmem],
        out_specs=vmem,
        scratch_shapes=[
            pltpu.VMEM((2, 2, two, width), bf16),
            pltpu.VMEM((2, img_rows, width), bf16),
            pltpu.VMEM((units, width), bf16),
            pltpu.VMEM((units, width), bf16),
            pltpu.VMEM((2, two, width), bf16),
            pltpu.VMEM((2, two, width), bf16),
            pltpu.VMEM((2, img_rows, width), f32),
            pltpu.VMEM((2, img_rows, width), bf16),
            pltpu.VMEM((2, img_rows, width), bf16),
            pltpu.SemaphoreType.DMA((loads,)),
            pltpu.SemaphoreType.DMA((4,)),
            pltpu.SemaphoreType.DMA((4,)),
        ],
        compiler_params=pltpu.CompilerParams(
            collective_id=1, has_side_effects=True, vmem_limit_bytes=VMEM_BYTES
        ),
    )(*operands, parts, w_final)


def fast(
    img_state,
    txt_state,
    cond_vec,
    text_len,
    latent,
    w_mod,
    w_qkv_img,
    w_qkv_txt,
    w_attn_out,
    w_up,
    w_down,
    w_final,
):
    prompts = img_state.shape[1]
    img_rows = img_state.shape[2]
    txt_rows = txt_state.shape[2]
    width = img_state.shape[3]
    parts = modulation(cond_vec[0], w_mod)
    own = [
        after(jnp.concatenate([img_state[0, p], txt_state[0, p]], axis=0), parts)
        for p in range(prompts)
    ]
    up = lax.all_gather(after(w_up, parts), ("cfg", "req"), axis=0, tiled=True)
    first = after(w_down, parts)
    downs = [first] + [flip(first, bits, "req") for bits in (1, 2, 3)]
    w_img = w_qkv_img.reshape(-1, width)
    w_txt = w_qkv_txt.reshape(-1, width)
    me = lax.axis_index("seq")
    starts = jnp.stack([txt_rows * (me ^ r) for r in range(4)]).astype(jnp.int32)
    pieces = [[rows, flip(rows, 1)] for rows in own]
    near = project(
        [rows[r] for rows in pieces for r in (0, 1)],
        [p for p in range(prompts) for r in (0, 1)],
        img_rows, parts, w_img, w_txt,
    )
    for p, rows in enumerate(pieces):
        rows.append(flip(after(rows[0], near[0]) if p else rows[0], 2))
    pieces[0].append(flip(pieces[0][2], 1))
    attended = []
    for p in range(prompts):
        if p == 0:
            starts = after(starts, downs[1:3])
        else:
            starts = after(starts, downs[3])
            pieces[p].append(flip(after(pieces[p][2], attended[0]), 1))
        far = project(pieces[p][2:], [p, p], img_rows, parts, w_img, w_txt)
        attended.append(attention(p, text_len[0], starts, near, far, img_rows))
    downs += [flip(after(one, attended[0]) if at else one, 1, "cfg") for at, one in enumerate(downs)]
    outs = [w_attn_out, flip(w_attn_out, 1), flip(after(w_attn_out, attended[0]), 2)]
    outs.append(flip(outs[2], 1))
    normed, resids = [], []
    for p in range(prompts):
        heads = [after(attended[p], attended[-1]) if p == 0 else attended[p], flip(attended[p], 1), flip(attended[p], 2)]
        heads.append(flip(heads[2], 1))
        rows, resid = attn_out(p, heads, outs, pieces[p], parts, img_rows)
        normed.append(rows)
        resids.append(resid)
    branch_vel = tail(normed, resids, up, downs, parts, w_final)
    return guide(branch_vel, latent)


def guide(branch_vel, latent):
    half_width = latent.shape[2]
    branch_index = lax.axis_index("cfg")
    own_half = lax.dynamic_slice_in_dim(branch_vel, branch_index * half_width, half_width, 2)
    other_half = lax.dynamic_slice_in_dim(
        branch_vel, (1 - branch_index) * half_width, half_width, 2
    )
    partner = partner_2(other_half.astype(jnp.bfloat16), "cfg", 0).astype(other_half.dtype)
    first = branch_index == 0
    cond_vel = jnp.where(first, own_half, partner)
    uncond_vel = jnp.where(first, partner, own_half)
    velocity = uncond_vel + 4.5 * (cond_vel - uncond_vel)
    latent_next = latent - 0.04 * velocity
    return (velocity, latent_next)


def plan(*shards):
    img_state, txt_state, w_qkv_img = shards[0], shards[1], shards[6]
    fits = (
        lax.axis_size("seq") == 4
        and lax.axis_size("req") == 4
        and lax.axis_size("cfg") == 2
        and img_state.shape[1] == 2
        and shards[9].shape[0] % 16 == 0
        and img_state.shape[2] % 128 == 0
        and txt_state.shape[2] % 16 == 0
        and w_qkv_img.shape[1] % (2 * HEAD) == 0
    )
    return fast(*shards) if fits else local(*shards)


def solution(mesh):
    placed = (
        P("cfg", "req", "seq", None),
        P("cfg", "req", "seq", None),
        P("cfg", None, None),
        P("cfg", "req"),
        P("req", "seq", "cfg"),
        P(("req", "seq"), None),
        P(None, "seq", None),
        P(None, "seq", None),
        P("seq", None),
        P(("cfg", "req", "seq"), None),
        P(("cfg", "req", "seq"), None),
        P(),
    )
    return jax.shard_map(
        plan,
        mesh=mesh,
        in_specs=placed,
        out_specs=(P("req", "seq", "cfg"), P("req", "seq", "cfg")),
        check_vma=False,
    )
```
